128 devices in a mesh: tile: 64 (over y, x_hi, z, core), comp: 2 (over x_lo).
Axes of the slice: x: 4 (x_hi: 2, x_lo: 2; x = x_hi * 2 + x_lo), y: 4, z: 4, core: 2. Of those that a mesh axis runs over, the one named last changes fastest.
Arguments:
- atm_state: bfloat16 [256, 1024, 256], P('comp', 'tile')
- ocean_state: bfloat16 [256, 32768], P('comp', 'tile')
- ocean_count: int32 [64], P('tile'), may hold values from 1 to 4, as said below
- regrid_src: int32 [2048, 2], P('tile'), may hold values from 0 to 255, as said below
- regrid_w: bfloat16 [2048, 2, 128, 128], P('tile'), may hold values from -0.375 to 0.375
- dw_kernel: float32 [9, 256], P(None, 'comp'), may hold values from -2.5 to 2.5
- atm_gain: bfloat16 [256], P('comp'), may hold values from 0.099609375 to 1.8984375
- atm_up: bfloat16 [256, 1024], P(None, 'comp'), may hold values from -0.375 to 0.375
- atm_down: bfloat16 [1024, 256], P('comp'), may hold values from -0.1875 to 0.1875
- ocean_gain: bfloat16 [256], P('comp'), may hold values from 0.099609375 to 1.8984375
- ocean_up: bfloat16 [256, 1024], P(None, 'comp'), may hold values from -0.375 to 0.375
- ocean_down: bfloat16 [1024, 256], P('comp'), may hold values from -0.1875 to 0.1875
Outputs:
- atm_out: bfloat16 [256, 1024, 256], P('comp', 'tile')
- ocean_result: bfloat16 [256, 32768], P('comp', 'tile')
The draws below stay inside these ranges and needn't reach their ends.
Inputs may be any that keep to these rules, and one draw needn't show every extreme that they name: Tile slots s < ocean_count[t] of tile index t hold ocean, the rest land; some entry equals 4. `regrid_src`: every entry names a live ocean slot g, whose tile index g // 4 differs by at most 2 from the tile index r // 32 of its block r.
All inputs are finite; a program needn't handle non-finite values.
Results may differ from the reference program's by a relative error of at most 0.012.
Values may be sent and summed in bfloat16 or wider, within the bound.
No kernel may reach another device: no remote copies, remote signals or barrier semaphores. Data moves between devices by JAX's collectives and lax.ppermute only.
A program may use at most 64 MiB of HBM per device.

```python
import jax
import jax.numpy as jnp
from jax import lax

CHANNEL_COUNT = 256
H = 1024
AR = 16
AW = 256
CELLS_PER_TILE = 128
MAXT = 4
K = 2
REACH = 2
NB = 32
NBT = 2048
NAR = 1024
TOTAL_SLOTS = 256
N_TILE = 64


def field_scales(key, array_shape, ratio):
    first, second = jax.random.split(key)
    lead = (array_shape[0],) + (1,) * (len(array_shape) - 1)
    rest = (1,) + tuple(array_shape[1:])
    channel = jnp.exp(jax.random.uniform(first, lead, jnp.float32, -1.0, 1.0) * jnp.log(ratio) * 0.5)
    cell = jnp.exp(jax.random.uniform(second, rest, jnp.float32, -1.0, 1.0) * jnp.log(ratio) * 0.25)
    return channel * cell


def tile_counts(key):
    key = jax.random.fold_in(key, 11)
    first, second, third = jax.random.split(key, 3)
    counts = jnp.minimum(jax.random.randint(first, (N_TILE,), 1, MAXT + 1), jax.random.randint(second, (N_TILE,), 1, MAXT + 1))
    chosen = jax.random.randint(third, (), 0, N_TILE)
    index = jnp.arange(N_TILE)
    full = (index == chosen) | (index == N_TILE - 1)
    return jnp.where(full, MAXT, counts).astype(jnp.int32)


def draw_atm_state(key, part):
    key = jax.random.fold_in(key, 1)
    first, second = jax.random.split(key)
    array_shape = (CHANNEL_COUNT, NAR, AW)
    base = jax.random.normal(first, array_shape, jnp.float32)
    ratio = 10.0
    return (base * field_scales(second, array_shape, ratio)).astype(jnp.bfloat16)


def draw_ocean_state(key, part):
    key = jax.random.fold_in(key, 2)
    first, second = jax.random.split(key)
    array_shape = (CHANNEL_COUNT, TOTAL_SLOTS * CELLS_PER_TILE)
    base = jax.random.normal(first, array_shape, jnp.float32)
    ratio = 10.0
    return (base * field_scales(second, array_shape, ratio)).astype(jnp.bfloat16)


def draw_ocean_count(key, part):
    counts = tile_counts(key)
    return counts


def draw_regrid_src(key, part):
    counts = tile_counts(key)
    key = jax.random.fold_in(key, 5)
    first, second = jax.random.split(key)
    rows = jnp.arange(NBT, dtype=jnp.int32)[:, None]
    member = jnp.arange(K, dtype=jnp.int32)[None, :]
    own_tile = rows // NB
    flat = rows % NB * K + member
    offsets = jax.random.randint(first, (NBT, K), -REACH, REACH + 1)
    offsets = jnp.where(flat < 2 * REACH + 1, flat - REACH, offsets)
    last_entry = (rows == NBT - 1) & (member == K - 1)
    offsets = jnp.where(last_entry, 0, offsets)
    owner = jnp.clip(own_tile + offsets, 0, N_TILE - 1)
    slot = jax.random.randint(second, (NBT, K), 0, 1 << 20) % counts[owner]
    first_entry = (rows == 0) & (member == 0)
    slot = jnp.where(first_entry, 0, slot)
    slot = jnp.where(last_entry, MAXT - 1, slot)
    return (owner * MAXT + slot).astype(jnp.int32)


def block_levels(stream_key, dims, shards, smallest, top_value):
    loudness, own = 1.0, jax.random.fold_in(stream_key, 6)
    for dim, blocks in shards:
        heights = jnp.exp(jax.random.uniform(jax.random.fold_in(own, dim), (blocks,), jnp.float32, smallest / len(shards), top_value / len(shards)))
        loudness = loudness * jnp.repeat(heights, dims[dim] // blocks).reshape([-1 if axis == dim else 1 for axis in range(len(dims))])
    return loudness


def normal_values(own_key, dims, scale, most, cuts=(), kind=jnp.bfloat16):
    level = block_levels(own_key, dims, cuts, -0.22, 0.18) if cuts else 1.0
    entries = jax.random.normal(own_key, dims, jnp.float32) * scale * level
    return jnp.minimum(jnp.maximum(entries, -most), most).astype(kind)


def setup_inputs(seed: int = 0) -> dict:
    splits = jax.random.split(jax.random.key(seed), 13)
    atm_state = draw_atm_state(jax.random.fold_in(splits[12], 71), 0)
    ocean_state = draw_ocean_state(jax.random.fold_in(splits[12], 71), 0)
    ocean_count = draw_ocean_count(jax.random.fold_in(splits[12], 71), 0)
    regrid_src = draw_regrid_src(jax.random.fold_in(splits[12], 71), 0)
    regrid_w = normal_values(splits[4], (NBT, K, CELLS_PER_TILE, CELLS_PER_TILE), (K * CELLS_PER_TILE) ** -0.5, 0.375, ((0, 64),))
    dw_kernel = normal_values(splits[5], (9, CHANNEL_COUNT), 0.35, 2.5, ((1, 2),), jnp.float32)
    atm_gain = jnp.clip(1.0 + 0.18 * jax.random.normal(splits[6], (CHANNEL_COUNT,), jnp.float32), 0.099609375, 1.8984375).astype(jnp.bfloat16)
    atm_up = normal_values(splits[7], (CHANNEL_COUNT, H), CHANNEL_COUNT ** -0.5, 0.375, ((1, 2),))
    atm_down = normal_values(splits[8], (H, CHANNEL_COUNT), H ** -0.5, 0.1875, ((0, 2),))
    ocean_gain = jnp.clip(1.0 + 0.18 * jax.random.normal(splits[9], (CHANNEL_COUNT,), jnp.float32), 0.099609375, 1.8984375).astype(jnp.bfloat16)
    ocean_up = normal_values(splits[10], (CHANNEL_COUNT, H), CHANNEL_COUNT ** -0.5, 0.375, ((1, 2),))
    ocean_down = normal_values(splits[11], (H, CHANNEL_COUNT), H ** -0.5, 0.1875, ((0, 2),))
    return {"atm_state": atm_state, "ocean_state": ocean_state, "ocean_count": ocean_count, "regrid_src": regrid_src, "regrid_w": regrid_w, "dw_kernel": dw_kernel, "atm_gain": atm_gain, "atm_up": atm_up, "atm_down": atm_down, "ocean_gain": ocean_gain, "ocean_up": ocean_up, "ocean_down": ocean_down}


def expand(weight, values):
    return jnp.dot(weight.T, values, preferred_element_type=jnp.float32)

def normalize(values, total, squares, gain):
    center = total / CHANNEL_COUNT
    spread = squares / CHANNEL_COUNT - center * center
    scaled = (values - center) * lax.rsqrt(spread + 1e-06) * gain.astype(jnp.float32)[:, None]
    return scaled.astype(jnp.bfloat16)

def mixed(values, gain, up_weight, down_weight):
    normed = normalize(values, lax.optimization_barrier(jnp.sum(values, 0)), lax.optimization_barrier(jnp.sum(values * values, 0)), gain)
    hidden = jax.nn.gelu(expand(up_weight, normed)).astype(jnp.bfloat16)
    return expand(down_weight, hidden)

def depthwise(pair):
    plane, weights = pair
    plane = plane.astype(jnp.float32)
    padded = jnp.pad(plane, ((1, 1), (0, 0)))
    height = plane.shape[0]
    result = jnp.zeros(plane.shape, jnp.float32)
    for lift in range(3):
        for turn in (-1, 0, 1):
            result = result + weights[lift * 3 + turn + 1] * jnp.roll(padded[lift:lift + height, :], -turn, axis=1)
    return result

def reference(atm_state, ocean_state, ocean_count, regrid_src, regrid_w, dw_kernel, atm_gain, atm_up, atm_down, ocean_gain, ocean_up, ocean_down):
    ocean_input = ocean_state.astype(jnp.float32)
    ocean_delta = mixed(ocean_input, ocean_gain, ocean_up, ocean_down)
    ocean_column = jnp.arange(TOTAL_SLOTS * CELLS_PER_TILE, dtype=jnp.int32)
    live = ocean_column // CELLS_PER_TILE % MAXT < ocean_count[ocean_column // (CELLS_PER_TILE * MAXT)]
    ocean_result = jnp.where(live[None, :], ocean_input + ocean_delta, 0.0).astype(jnp.bfloat16)
    conv = lax.map(depthwise, (atm_state, dw_kernel.T))
    cells = AR * AW
    conv_flat = conv.reshape(CHANNEL_COUNT, NAR * AW)
    state_flat = atm_state.reshape(CHANNEL_COUNT, NAR * AW)
    every_slab = ocean_result.reshape(CHANNEL_COUNT, TOTAL_SLOTS, CELLS_PER_TILE)

    def one_tile(index):
        first = (index * cells).astype(jnp.int32)
        block = lax.dynamic_slice_in_dim(conv_flat, first, cells, 1)
        delta = mixed(block, atm_gain, atm_up, atm_down)
        row_first = (index * NB).astype(jnp.int32)
        sources = lax.dynamic_slice_in_dim(regrid_src, row_first, NB, 0)
        weights = lax.dynamic_slice_in_dim(regrid_w, row_first, NB, 0)
        gathered = jnp.take(every_slab, sources.reshape(-1), axis=1).reshape(CHANNEL_COUNT, NB, K, CELLS_PER_TILE)
        regrid = jnp.einsum('bkpq,cbkq->cbp', weights.astype(jnp.float32), gathered.astype(jnp.float32)).reshape(CHANNEL_COUNT, cells)
        state = lax.dynamic_slice_in_dim(state_flat, first, cells, 1).astype(jnp.float32)
        return (state + delta + regrid).astype(jnp.bfloat16)
    blocks = lax.map(one_tile, jnp.arange(N_TILE, dtype=jnp.int32))
    atm_out = jnp.transpose(blocks, (1, 0, 2)).reshape(CHANNEL_COUNT, NAR, AW)
    return (atm_out, ocean_result)
```

```python
import functools

import jax
import jax.numpy as jnp
from jax import lax
from jax.experimental import pallas as pl
from jax.experimental.pallas import tpu as pltpu
from jax.sharding import PartitionSpec as P

CHANNELS = 256
HALF = 128
ROWS = 16
COLS = 256
LANES = 128
CELLS_PER_TILE = 128
SLOTS = 4
F32 = jnp.float32
BF16 = jnp.bfloat16
AXES = ("tile", "comp")
WHOLE = pl.BlockSpec()
SMEM = pl.BlockSpec(memory_space=pltpu.SMEM)
SENT = ((3, 9), (1, 3))
MIXED = ((4, 8), (0, 4))


def sds(shape, dtype=BF16):
    return jax.ShapeDtypeStruct(shape, dtype)


def call(kernel, out, ins, specs, scratch=(), flops=0, moved=1 << 20, name=None, **kw):
    return pl.pallas_call(
        kernel,
        out_shape=out,
        in_specs=specs,
        out_specs=kw.pop("out_specs", jax.tree.map(lambda _: WHOLE, out)),
        scratch_shapes=list(scratch),
        compiler_params=pltpu.CompilerParams(vmem_limit_bytes=60 << 20),
        cost_estimate=pl.CostEstimate(flops=flops, bytes_accessed=moved, transcendentals=0),
        name=name,
        **kw,
    )(*ins)


def side_of():
    return lax.axis_index("comp")


def row_at(j, side):
    return jnp.where(side == 0, j, ROWS - 1 - j)


def prep_kernel(state, taps, atm_gain, ocean_gain, *rest):
    sends, (head, keep, own_p, tall) = rest[: len(SENT)], rest[len(SENT) :]
    side = side_of()
    gains = [g[...].astype(F32).reshape(1, HALF) for g in (atm_gain, ocean_gain)]
    own_p[...] = jnp.concatenate([taps[...], *gains, jnp.zeros((5, HALF), F32)], 0)
    high = own_p[...].astype(BF16)
    low = (own_p[...] - high.astype(F32)).astype(BF16)
    head[HALF:, :LANES] = high
    head[HALF:, LANES:] = low
    for h in range(2):
        part = state[:, :, h * LANES : (h + 1) * LANES].astype(F32)
        tall[h] = part.reshape(HALF * ROWS, LANES)

    def row(r):
        parts = [tall.at[h][pl.ds(r, HALF, stride=ROWS), :] for h in range(2)]
        return jnp.concatenate(parts, 1).astype(BF16)

    for j in range(9):
        keep[j] = row(row_at(j, side))
        away = row(row_at(j, 1 - side))
        if j == 0:
            head[:HALF, :] = away
        for (first, last), sent in zip(SENT, sends):
            if first <= j < last:
                sent[j - first] = away


def params_of(head):
    return head[HALF:, :LANES].astype(F32) + head[HALF:, LANES:].astype(F32)


def gelu(x):
    inner = x * (0.7978845608028654 + 0.035677408136300125 * (x * x))
    return (x * (0.5 + 0.5 * jnp.tanh(inner))).astype(BF16)


def dot(a, b):
    return jnp.dot(a, b, preferred_element_type=F32)


def normed(values, gains):
    total = sum(jnp.sum(v, 0, keepdims=True) for v in values)
    squares = sum(jnp.sum(v * v, 0, keepdims=True) for v in values)
    center = total / CHANNELS
    spread = squares / CHANNELS - center * center
    scale = lax.rsqrt(spread + 1e-06)
    return [((v - center) * scale * g).astype(BF16) for v, g in zip(values, gains)]


def turned_up(up, j, side):
    halves = [up[pl.ds(pl.multiple_of(s * HALF, HALF), HALF), j * 256 : (j + 1) * 256] for s in (side, 1 - side)]
    return jnp.concatenate(halves, 0).T


def turned_down(down, j, side):
    halves = [down[j * 256 : (j + 1) * 256, pl.ds(pl.multiple_of(s * HALF, HALF), HALF)] for s in (side, 1 - side)]
    return jnp.concatenate(halves, 1).T


def ocean_kernel(mine, theirs, own_p, head, keep, up, down, kept, sent, pair, x):
    side = side_of()
    pair[0] = keep[0]
    pair[1] = head[:HALF, :]
    gains = [own_p[...].T[:, 10:11], params_of(head).T[:, 10:11]]
    own, other = normed([mine[...].astype(F32), theirs[...].astype(F32)], gains)
    x[:HALF, :] = own
    x[HALF:, :] = other
    total = None
    for j in range(2):
        hidden = gelu(dot(turned_up(up, j, side), x[...]))
        part = dot(turned_down(down, j, side), hidden)
        total = part if total is None else total + part
    kept[...] = total[:HALF]
    sent[...] = total[HALF:].astype(BF16)


def ocean_result_kernel(count, state, kept, got, result, slots):
    for s in range(SLOTS):
        cells = slice(s * CELLS_PER_TILE, (s + 1) * CELLS_PER_TILE)
        value = state[:, cells].astype(F32) + (kept[:, cells] + got[:, cells].astype(F32))
        value = jnp.where(s < count[0], value, 0.0).astype(BF16)
        result[:, cells] = value
        slots[s] = value


def mix(rows, where_own, where_other, ins, own_p, head, blocks, kept, sent, x):
    side = side_of()
    params = []
    for taps in (own_p[...], params_of(head)):
        flipped = jnp.concatenate([taps[6:9], taps[3:6], taps[0:3], taps[9:]], 0)
        params.append(jnp.where(side == 0, taps, flipped).T)

    def fetch(place):
        ref, index = place
        value = ins[ref][:HALF, :] if index is None else ins[ref][index]
        return value.astype(F32)

    def conv(places, p):
        lines = [fetch(place) for place in places]
        left, middle, right = [
            sum(p[:, 3 * a + b : 3 * a + b + 1] * lines[a] for a in range(3)) for b in range(3)
        ]
        return middle + pltpu.roll(left, 1, 1) + pltpu.roll(right, COLS - 1, 1)

    for i in range(rows):
        values = [conv(where_own[i : i + 3], params[0]), conv(where_other[i : i + 3], params[1])]
        own, other = normed(values, [p[:, 9:10] for p in params])
        x[:HALF, i * COLS : (i + 1) * COLS] = own
        x[HALF:, i * COLS : (i + 1) * COLS] = other
    for i in range(0, rows, 2):
        cells = slice(i * COLS, (i + 2) * COLS)
        delta = None
        for j in range(4):
            part = dot(blocks[4 + j], gelu(dot(blocks[j], x[:, cells])))
            delta = part if delta is None else delta + part
        for n in range(2):
            value = delta[:, n * COLS : (n + 1) * COLS].astype(BF16)
            kept[i + n] = value[:HALF]
            sent[i + n] = value[HALF:]


def mix_first_kernel(rows, where_own, where_other, n_in, own_p, head, up, down, got_up, got_down, *rest):
    ins, (kept, sent, blocks, x) = rest[:n_in], rest[n_in:]
    side = side_of()
    for n, (u, d) in enumerate(((up, down), (got_up, got_down))):
        for j in range(2):
            blocks[2 * n + j] = turned_up(u, j, side)
            blocks[4 + 2 * n + j] = turned_down(d, j, side)
    mix(rows, where_own, where_other, ins, own_p, head, blocks, kept, sent, x)


def mix_kernel(rows, where_own, where_other, n_in, own_p, head, blocks, *rest):
    ins, (kept, sent, x) = rest[:n_in], rest[n_in:]
    mix(rows, where_own, where_other, ins, own_p, head, blocks, kept, sent, x)


def regrid_kernel(source, table_own, table_swap, table_e1, table_e2, table_last, w, out, table):
    step = pl.program_id(0)
    tile = lax.axis_index("tile")
    core, odd = lax.rem(tile, 2), lax.rem(tile // 2, 2)

    @pl.when(step == 0)
    def _():
        for n, part in enumerate((table_own, table_swap, table_last, table_e1, table_e2)):
            table[n * SLOTS : (n + 1) * SLOTS] = part[...]

    def slab(b, k):
        slot = source[b, k]
        offset = slot // SLOTS - tile
        near = jnp.where((offset > 0) == (core == 0), 1, 2)
        far = jnp.where((offset > 0) == (odd == 1), 3, 4)
        part = jnp.where(offset == 0, 0, jnp.where(abs(offset) == 1, near, far))
        return table[part * SLOTS + lax.rem(slot, SLOTS)]

    per_step = w.shape[0]
    for n in range(per_step):
        b = step * per_step + n
        slabs = jnp.concatenate([slab(b, 0), slab(b, 1)], 1)
        weight = jnp.concatenate([w[n, 0], w[n, 1]], 1)
        value = lax.dot_general(slabs, weight, (((1,), (1,)), ((), ())), preferred_element_type=F32)
        out[n // 2, :, (n % 2) * 128 : (n % 2 + 1) * 128] = value


def final_kernel(n, state, regrid, *rest):
    kept, got, out, tall = rest[:n], rest[n : 2 * n], rest[2 * n], rest[2 * n + 1]
    side = side_of()
    depth = state.shape[0]
    for refs, which in ((kept, side), (got, 1 - side)):
        for (first, last), ref in zip(MIXED, refs):
            for j in range(first, last):
                r = row_at(j, which)
                value = regrid[r] + ref[j - first].astype(F32)
                for h in range(2):
                    tall.at[h][pl.ds(r, depth, stride=ROWS), :] = value[:, h * LANES : (h + 1) * LANES]
    for h in range(2):
        lanes = slice(h * LANES, (h + 1) * LANES)
        added = tall[h].reshape(depth, ROWS, LANES)
        out[:, :, lanes] = (state[:, :, lanes].astype(F32) + added).astype(BF16)


def on_device(
    atm_state, ocean_state, ocean_count, regrid_src, regrid_w, dw_kernel,
    atm_gain, atm_up, atm_down, ocean_gain, ocean_up, ocean_down,
):
    tiles = lax.axis_size("tile")
    tile = lax.axis_index("tile")

    def move(x, to):
        route = []
        for t in range(tiles):
            for c in range(2):
                u, d = to(t, c)
                if 0 <= u < tiles:
                    route.append((t * 2 + c, u * 2 + d))
        return lax.ppermute(x, AXES, route)

    def partner(x):
        return move(x, lambda t, c: (t, 1 - c))

    half_turn = 8 if tiles >= 16 else 0

    def across(x):
        return move(x, lambda t, c: (t ^ half_turn, 1 - c))

    ocean_theirs = partner(ocean_state)
    got_up, got_down = across(atm_up), across(atm_down)
    *sends, head_sent, keep, own_p = call(
        prep_kernel,
        [sds((b - a, HALF, COLS)) for a, b in SENT]
        + [sds((HALF + 16, COLS)), sds((9, HALF, COLS)), sds((16, HALF), F32)],
        (atm_state, dw_kernel, atm_gain, ocean_gain),
        [WHOLE] * 4,
        [pltpu.VMEM((2, HALF * ROWS, LANES), F32)],
        moved=3 << 20,
        name="prep",
    )
    head = partner(head_sent)
    got = [partner(s) for s in sends]

    cells = ocean_state.shape[1]
    ocean_kept, ocean_sent, pair = call(
        ocean_kernel,
        [sds((HALF, cells), F32), sds((HALF, cells)), sds((2, HALF, COLS))],
        (ocean_state, ocean_theirs, own_p, head, keep, ocean_up, ocean_down),
        [WHOLE] * 7,
        [pltpu.VMEM((256, cells), BF16)],
        flops=2 * 2 * 256 * 512 * cells,
        moved=2 << 20,
        name="ocean",
    )
    ocean_got = partner(ocean_sent)
    edges = move(pair, lambda t, c: (t - 1 + 2 * c, 1 - c))
    ocean_result, slots = call(
        ocean_result_kernel,
        [sds((HALF, cells)), sds((SLOTS, HALF, CELLS_PER_TILE))],
        (ocean_count, ocean_state, ocean_kept, ocean_got),
        [SMEM, WHOLE, WHOLE, WHOLE],
        moved=1 << 20,
        name="ocean_result",
    )
    swapped = move(slots, lambda t, c: (t ^ 1, c))
    e2 = move(slots, lambda t, c: (t ^ 2, c))
    e1 = move(slots, lambda t, c: (t + 2 if t // 2 % 2 else t - 2, c))
    passed = jnp.where(tile % 2 == tile // 2 % 2, e2, e1)
    last = move(passed, lambda t, c: (t ^ 1, c))

    kept_rows, got_rows, blocks = [], [], None
    for a, b in MIXED:
        ins, where_own, where_other = [keep], [], []
        for j in range(a - 1, b + 1):
            if j < 0:
                where_own.append((len(ins), 1))
                where_other.append((len(ins), 0))
                ins.append(edges)
                continue
            where_own.append((0, j))
            if j == 0:
                where_other.append((len(ins), None))
                ins.append(head)
                continue
            k = [n for n, (p, q) in enumerate(SENT) if p <= j < q][0]
            place = [n for n, x in enumerate(ins) if x is got[k]]
            if not place:
                place = [len(ins)]
                ins.append(got[k])
            where_other.append((place[0], j - SENT[k][0]))
        rows = b - a
        cost = dict(flops=rows * COLS * 256 * 1024 * 4, moved=3 << 20)
        out = [sds((rows, HALF, COLS))] * 2
        x_spec = pltpu.VMEM((CHANNELS, rows * COLS), BF16)
        if blocks is None:
            kept, sent, blocks = call(
                functools.partial(mix_first_kernel, rows, where_own, where_other, len(ins)),
                out + [sds((8, 256, 256))],
                (own_p, head, atm_up, atm_down, got_up, got_down, *ins),
                [WHOLE] * (6 + len(ins)),
                [x_spec],
                name="mix_first",
                **cost,
            )
        else:
            kept, sent = call(
                functools.partial(mix_kernel, rows, where_own, where_other, len(ins)),
                out,
                (own_p, head, blocks, *ins),
                [WHOLE] * (3 + len(ins)),
                [x_spec],
                name="mix",
                **cost,
            )
        kept_rows.append(kept)
        got_rows.append(partner(sent))

    steps = 4
    per_step = regrid_src.shape[0] // steps
    table = pl.BlockSpec((SLOTS, HALF, CELLS_PER_TILE), lambda i: (0, 0, 0))
    regrid = call(
        regrid_kernel,
        sds((ROWS, HALF, COLS), F32),
        (regrid_src, slots, swapped, e1, e2, last, regrid_w),
        [SMEM] + [table] * 5 + [pl.BlockSpec((per_step, 2, 128, 128), lambda i: (i, 0, 0, 0))],
        [pltpu.VMEM((5 * SLOTS, HALF, CELLS_PER_TILE), BF16)],
        grid=(steps,),
        out_specs=pl.BlockSpec((ROWS // steps, HALF, COLS), lambda i: (i, 0, 0)),
        flops=32 * 2 * 128 * 256 * 128,
        moved=5 << 20,
        name="regrid",
    )
    depth = HALF // 4
    rows_spec = [pl.BlockSpec((b - a, depth, COLS), lambda i: (0, i, 0)) for a, b in MIXED]
    state_spec = pl.BlockSpec((depth, ROWS, COLS), lambda i: (i, 0, 0))
    atm_out = call(
        functools.partial(final_kernel, len(MIXED)),
        sds((HALF, ROWS, COLS)),
        (atm_state, regrid, *kept_rows, *got_rows),
        [state_spec, pl.BlockSpec((ROWS, depth, COLS), lambda i: (0, i, 0))] + rows_spec * 2,
        [pltpu.VMEM((2, depth * ROWS, LANES), F32)],
        grid=(HALF // depth,),
        out_specs=state_spec,
        moved=5 << 20,
        name="final",
    )
    return (atm_out, ocean_result)


def solution(mesh):
    return jax.shard_map(
        on_device,
        mesh=mesh,
        in_specs=(
            P("comp", "tile", None),
            P("comp", "tile"),
            P("tile"),
            P("tile", None),
            P("tile", None, None, None),
            P(None, "comp"),
            P("comp"),
            P(None, "comp"),
            P("comp", None),
            P("comp"),
            P(None, "comp"),
            P("comp", None),
        ),
        out_specs=(P("comp", "tile", None), P("comp", "tile")),
        check_vma=False,
    )
```

```python
import functools

import jax
import jax.numpy as jnp
from jax import lax
from jax.experimental import pallas as pl
from jax.experimental.pallas import tpu as pltpu
from jax.sharding import PartitionSpec as P

CHANNELS = 256
HALF = 128
ROWS = 16
COLS = 256
LANES = 128
CELLS_PER_TILE = 128
SLOTS = 4
F32 = jnp.float32
BF16 = jnp.bfloat16
AXES = ("tile", "comp")
WHOLE = pl.BlockSpec()
SMEM = pl.BlockSpec(memory_space=pltpu.SMEM)
ANY = pl.BlockSpec(memory_space=pl.ANY)
FINAL_STEPS = 4
SENT = ((3, 9), (1, 3))
MIXED = ((4, 8), (0, 4))


def sds(shape, dtype=BF16):
    return jax.ShapeDtypeStruct(shape, dtype)


def call(kernel, out, ins, specs, scratch=(), name=None, **kw):
    return pl.pallas_call(
        kernel,
        out_shape=out,
        in_specs=specs,
        out_specs=kw.pop("out_specs", jax.tree.map(lambda _: WHOLE, out)),
        scratch_shapes=list(scratch),
        compiler_params=pltpu.CompilerParams(vmem_limit_bytes=64 << 20),
        cost_estimate=pl.CostEstimate(flops=0, bytes_accessed=0, transcendentals=0),
        name=name,
        **kw,
    )(*ins)


def side_of():
    return lax.axis_index("comp")


def row_at(j, side):
    return jnp.where(side == 0, j, ROWS - 1 - j)


def taker(lines, side, take):
    out = lax.broadcasted_iota(jnp.int32, (lines * 16, 256), 0)
    into = lax.broadcasted_iota(jnp.int32, (lines * 16, 256), 1)
    hit = ((out & 15) == (into >> 4)) & ((into & 15) == take(out >> 4))
    return jnp.where(hit, 1.0, 0.0).astype(BF16)


def head_kernel(state, ocean, taps, atm_gain, ocean_gain, head, own_p):
    side = side_of()
    gains = [g[...].astype(F32).reshape(1, HALF) for g in (atm_gain, ocean_gain)]
    own_p[...] = jnp.concatenate([taps[...], *gains, jnp.zeros((5, HALF), F32)], 0)
    high = own_p[...].astype(BF16)
    low = (own_p[...] - high.astype(F32)).astype(BF16)
    head[384:, :LANES] = high
    head[384:, LANES:] = low
    head[:HALF, :] = ocean[:, :COLS]
    head[HALF : 2 * HALF, :] = ocean[:, COLS:]
    pick = taker(1, side, lambda n: row_at(0, 1 - side))
    for b in range(HALF // 16):
        block = state[16 * b : 16 * (b + 1)].reshape(256, COLS)
        head[2 * HALF + 16 * b : 2 * HALF + 16 * (b + 1), :] = dot(pick, block).astype(BF16)


def split_kernel(state, *rest):
    sends, keep = rest[: len(SENT)], rest[len(SENT)]
    side = side_of()
    pick = taker(17, side, lambda n: jnp.where(n < 9, row_at(n, side), row_at(n - 8, 1 - side)))
    for b in range(HALF // 16):
        channels = slice(16 * b, 16 * (b + 1))
        lines = dot(pick, state[channels].reshape(256, COLS)).astype(BF16)
        for j in range(9):
            keep[j, channels, :] = lines[16 * j : 16 * (j + 1)]
            for (first, last), sent in zip(SENT, sends):
                if first <= j < last:
                    sent[j - first, channels, :] = lines[16 * (j + 8) : 16 * (j + 9)]


def params_of(head):
    return head[384:, :LANES].astype(F32) + head[384:, LANES:].astype(F32)


def gelu(x):
    inner = x * (0.7978845608028654 + 0.035677408136300125 * (x * x))
    return (x * (0.5 + 0.5 * jnp.tanh(inner))).astype(BF16)


def dot(a, b):
    return jnp.dot(a, b, preferred_element_type=F32)


def normed(values, gains):
    total = sum(jnp.sum(v, 0, keepdims=True) for v in values)
    squares = sum(jnp.sum(v * v, 0, keepdims=True) for v in values)
    center = total / CHANNELS
    spread = squares / CHANNELS - center * center
    scale = lax.rsqrt(spread + 1e-06)
    return [((v - center) * scale * g).astype(BF16) for v, g in zip(values, gains)]


def turned_up(up, j, side):
    halves = [up[pl.ds(pl.multiple_of(s * HALF, HALF), HALF), j * 256 : (j + 1) * 256] for s in (side, 1 - side)]
    return jnp.concatenate(halves, 0).T


def turned_down(down, j, side):
    halves = [down[j * 256 : (j + 1) * 256, pl.ds(pl.multiple_of(s * HALF, HALF), HALF)] for s in (side, 1 - side)]
    return jnp.concatenate(halves, 1).T


def ocean_kernel(mine, own_p, head, keep, up, down, kept, sent, pair, x):
    side = side_of()
    pair[0] = keep[0]
    pair[1] = head[2 * HALF : 3 * HALF, :]
    gains = [own_p[...].T[:, 10:11], params_of(head).T[:, 10:11]]
    theirs = jnp.concatenate([head[:HALF, :], head[HALF : 2 * HALF, :]], 1)
    own, other = normed([mine[...].astype(F32), theirs.astype(F32)], gains)
    x[:HALF, :] = own
    x[HALF:, :] = other
    total = None
    for j in range(2):
        hidden = gelu(dot(turned_up(up, j, side), x[...]))
        part = dot(turned_down(down, j, side), hidden)
        total = part if total is None else total + part
    kept[...] = total[:HALF]
    sent[...] = total[HALF:].astype(BF16)


def ocean_result_kernel(count, state, kept, got, result, slots):
    for s in range(SLOTS):
        cells = slice(s * CELLS_PER_TILE, (s + 1) * CELLS_PER_TILE)
        value = state[:, cells].astype(F32) + (kept[:, cells] + got[:, cells].astype(F32))
        value = jnp.where(s < count[0], value, 0.0).astype(BF16)
        result[:, cells] = value
        slots[s] = value


def mix(rows, where_own, where_other, ins, own_p, head, blocks, kept, sent, x):
    side = side_of()
    params = []
    for taps in (own_p[...], params_of(head)):
        flipped = jnp.concatenate([taps[6:9], taps[3:6], taps[0:3], taps[9:]], 0)
        params.append(jnp.where(side == 0, taps, flipped).T)

    def fetch(place):
        ref, index = place
        value = ins[ref][2 * HALF : 3 * HALF, :] if index is None else ins[ref][index]
        return value.astype(F32)

    def conv(places, p):
        lines = [fetch(place) for place in places]
        left, middle, right = [
            sum(p[:, 3 * a + b : 3 * a + b + 1] * lines[a] for a in range(3)) for b in range(3)
        ]
        return middle + pltpu.roll(left, 1, 1) + pltpu.roll(right, COLS - 1, 1)

    for i in range(rows):
        values = [conv(where_own[i : i + 3], params[0]), conv(where_other[i : i + 3], params[1])]
        own, other = normed(values, [p[:, 9:10] for p in params])
        x[:HALF, i * COLS : (i + 1) * COLS] = own
        x[HALF:, i * COLS : (i + 1) * COLS] = other
    up = blocks[:4].reshape(4 * 256, CHANNELS)
    down = jnp.concatenate([blocks[4 + j] for j in range(4)], 1)
    for i in range(rows):
        hidden = gelu(dot(up, x[:, i * COLS : (i + 1) * COLS]))
        value = dot(down, hidden).astype(BF16)
        kept[i] = value[:HALF]
        sent[i] = value[HALF:]


def mix_first_kernel(rows, where_own, where_other, n_in, own_p, head, up, down, got_up, got_down, *rest):
    ins, (kept, sent, blocks, x) = rest[:n_in], rest[n_in:]
    side = side_of()
    for n, (u, d) in enumerate(((up, down), (got_up, got_down))):
        for j in range(2):
            blocks[2 * n + j] = turned_up(u, j, side)
            blocks[4 + 2 * n + j] = turned_down(d, j, side)
    mix(rows, where_own, where_other, ins, own_p, head, blocks, kept, sent, x)


def mix_kernel(rows, where_own, where_other, n_in, own_p, head, blocks, *rest):
    ins, (kept, sent, x) = rest[:n_in], rest[n_in:]
    mix(rows, where_own, where_other, ins, own_p, head, blocks, kept, sent, x)


def regrid_kernel(source, own, swap, e1, e2, swap_e1, swap_e2, w, later, out, table):
    step = pl.program_id(0)
    tile = lax.axis_index("tile")
    core, odd = lax.rem(tile, 2), lax.rem(tile // 2, 2)

    @pl.when(step == 0)
    def _():
        for n, part in enumerate((own, swap, e1, e2, swap_e1, swap_e2)):
            table[n * SLOTS : (n + 1) * SLOTS] = part[...]

    def slab(b, k):
        slot = source[k, b]
        offset = slot // SLOTS - tile
        up = offset > 0
        far = jnp.where(up == (odd == 1), 2, 3)
        part = jnp.where(abs(offset) == 1, jnp.where(up == (core == 0), 1, far + 2), far)
        part = jnp.where(offset == 0, 0, part)
        return table[part * SLOTS + lax.rem(slot, SLOTS)]

    per_step = w.shape[0]
    for n in range(per_step):
        b = step * per_step + n
        slabs = jnp.concatenate([slab(b, 0), slab(b, 1)], 1)
        weight = jnp.concatenate([w[n, 0], w[n, 1]], 1)
        value = lax.dot_general(slabs, weight, (((1,), (1,)), ((), ())), preferred_element_type=F32)
        out[n // 2, :, (n % 2) * 128 : (n % 2 + 1) * 128] = value.astype(BF16)


def final_kernel(n, state, regrid, *rest):
    kept, got, out = rest[:n], rest[n : 2 * n], rest[2 * n]
    side = side_of()
    place = taker(16, side, lambda n: jnp.where(n < 8, row_at(n, side), row_at(n - 8, 1 - side)))
    place = jnp.concatenate([place.T, taker(16, side, lambda n: n).T], 1)
    for b in range(state.shape[0] // 16):
        channels = slice(16 * b, 16 * (b + 1))
        lines = []
        for refs in (kept, got):
            for j in range(ROWS // 2):
                k = [n for n, (p, q) in enumerate(MIXED) if p <= j < q][0]
                lines.append(refs[k][j - MIXED[k][0], channels, :])
        lines += [regrid[r, channels, :] for r in range(ROWS)]
        added = dot(place, jnp.concatenate(lines, 0)).reshape(16, ROWS, COLS)
        out[channels] = (state[channels].astype(F32) + added).astype(BF16)


def on_device(
    atm_state, ocean_state, ocean_count, regrid_src, regrid_w, dw_kernel,
    atm_gain, atm_up, atm_down, ocean_gain, ocean_up, ocean_down,
):
    tiles = lax.axis_size("tile")

    def move(x, to):
        route = []
        for t in range(tiles):
            for c in range(2):
                u, d = to(t, c)
                if 0 <= u < tiles:
                    route.append((t * 2 + c, u * 2 + d))
        return lax.ppermute(x, AXES, route)

    def partner(x):
        return move(x, lambda t, c: (t, 1 - c))

    half_turn = 8 if tiles >= 16 else 0

    def across(x):
        return move(x, lambda t, c: (t ^ half_turn, 1 - c))

    got_up, got_down = across(atm_up), across(atm_down)
    head_sent, own_p = call(
        head_kernel,
        [sds((3 * HALF + 16, COLS)), sds((16, HALF), F32)],
        (atm_state, ocean_state, dw_kernel, atm_gain, ocean_gain),
        [WHOLE] * 5,
        name="head",
    )
    head = partner(head_sent)
    *sends, keep = call(
        split_kernel,
        [sds((b - a, HALF, COLS)) for a, b in SENT] + [sds((9, HALF, COLS))],
        (atm_state,),
        [WHOLE],
        name="split",
    )
    got = [partner(s) for s in sends]

    cells = ocean_state.shape[1]
    ocean_kept, ocean_sent, pair = call(
        ocean_kernel,
        [sds((HALF, cells), F32), sds((HALF, cells)), sds((2, HALF, COLS))],
        (ocean_state, own_p, head, keep, ocean_up, ocean_down),
        [WHOLE] * 6,
        [pltpu.VMEM((256, cells), BF16)],
        name="ocean",
    )
    ocean_got = partner(ocean_sent)
    edges = move(pair, lambda t, c: (t - 1 + 2 * c, 1 - c))
    ocean_result, slots = call(
        ocean_result_kernel,
        [sds((HALF, cells)), sds((SLOTS, HALF, CELLS_PER_TILE))],
        (ocean_count, ocean_state, ocean_kept, ocean_got),
        [SMEM, WHOLE, WHOLE, WHOLE],
        name="ocean_result",
    )
    swapped = move(slots, lambda t, c: (t ^ 1, c))
    e2 = move(slots, lambda t, c: (t ^ 2, c))
    e1 = move(slots, lambda t, c: (t + 2 if t // 2 % 2 else t - 2, c))
    swap_e1, swap_e2 = [move(e, lambda t, c: (t ^ 1, c)) for e in (e1, e2)]

    kept_rows, got_rows, blocks = [], [], None
    for a, b in MIXED:
        ins, where_own, where_other = [keep], [], []
        for j in range(a - 1, b + 1):
            if j < 0:
                where_own.append((len(ins), 1))
                where_other.append((len(ins), 0))
                ins.append(edges)
                continue
            where_own.append((0, j))
            if j == 0:
                where_other.append((len(ins), None))
                ins.append(head)
                continue
            k = [n for n, (p, q) in enumerate(SENT) if p <= j < q][0]
            place = [n for n, x in enumerate(ins) if x is got[k]]
            if not place:
                place = [len(ins)]
                ins.append(got[k])
            where_other.append((place[0], j - SENT[k][0]))
        rows = b - a
        out = [sds((rows, HALF, COLS))] * 2
        x_spec = pltpu.VMEM((CHANNELS, rows * COLS), BF16)
        if blocks is None:
            kept, sent, blocks = call(
                functools.partial(mix_first_kernel, rows, where_own, where_other, len(ins)),
                out + [sds((8, 256, 256))],
                (own_p, head, atm_up, atm_down, got_up, got_down, *ins),
                [WHOLE] * (6 + len(ins)),
                [x_spec],
                name="mix_first",
            )
        else:
            kept, sent = call(
                functools.partial(mix_kernel, rows, where_own, where_other, len(ins)),
                out,
                (own_p, head, blocks, *ins),
                [WHOLE] * (3 + len(ins)),
                [x_spec],
                name="mix",
            )
        kept_rows.append(kept)
        got_rows.append(partner(sent))

    steps = 4
    per_step = regrid_src.shape[0] // steps
    table = pl.BlockSpec((SLOTS, HALF, CELLS_PER_TILE), lambda i: (0, 0, 0))
    regrid = call(
        regrid_kernel,
        sds((ROWS, HALF, COLS)),
        (regrid_src.T, slots, swapped, e1, e2, swap_e1, swap_e2, regrid_w, got_rows[0]),
        [SMEM] + [table] * 6 + [pl.BlockSpec((per_step, 2, 128, 128), lambda i: (i, 0, 0, 0)), ANY],
        [pltpu.VMEM((6 * SLOTS, HALF, CELLS_PER_TILE), BF16)],
        grid=(steps,),
        out_specs=pl.BlockSpec((ROWS // steps, HALF, COLS), lambda i: (i, 0, 0)),
        name="regrid",
    )
    depth = HALF // FINAL_STEPS
    rows_spec = [pl.BlockSpec((b - a, depth, COLS), lambda i: (0, i, 0)) for a, b in MIXED]
    state_spec = pl.BlockSpec((depth, ROWS, COLS), lambda i: (i, 0, 0))
    atm_out = call(
        functools.partial(final_kernel, len(MIXED)),
        sds((HALF, ROWS, COLS)),
        (atm_state, regrid, *kept_rows, *got_rows),
        [state_spec, pl.BlockSpec((ROWS, depth, COLS), lambda i: (0, i, 0))] + rows_spec * 2,
        grid=(FINAL_STEPS,),
        out_specs=state_spec,
        name="final",
    )
    return (atm_out, ocean_result)


def solution(mesh):
    return jax.shard_map(
        on_device,
        mesh=mesh,
        in_specs=(
            P("comp", "tile", None),
            P("comp", "tile"),
            P("tile"),
            P("tile", None),
            P("tile", None, None, None),
            P(None, "comp"),
            P("comp"),
            P(None, "comp"),
            P("comp", None),
            P("comp"),
            P(None, "comp"),
            P("comp", None),
        ),
        out_specs=(P("comp", "tile", None), P("comp", "tile")),
        check_vma=False,
    )
```

```python
import functools

import jax
import jax.numpy as jnp
from jax import lax
from jax.experimental import pallas as pl
from jax.experimental.pallas import tpu as pltpu
from jax.sharding import PartitionSpec as P

CHANNELS = 256
HALF = 128
ROWS = 16
COLS = 256
LANES = 128
CELLS_PER_TILE = 128
SLOTS = 4
F32 = jnp.float32
BF16 = jnp.bfloat16
AXES = ("tile", "comp")
WHOLE = pl.BlockSpec()
SMEM = pl.BlockSpec(memory_space=pltpu.SMEM)
ANY = pl.BlockSpec(memory_space=pl.ANY)
FINAL_STEPS = 2
OCEAN_COST = 8 * 10**9
SENT = ((3, 9), (1, 3))
MIXED = ((4, 8), (0, 4))


def sds(shape, dtype=BF16):
    return jax.ShapeDtypeStruct(shape, dtype)


def call(kernel, out, ins, specs, scratch=(), name=None, flops=0, **kw):
    return pl.pallas_call(
        kernel,
        out_shape=out,
        in_specs=specs,
        out_specs=kw.pop("out_specs", jax.tree.map(lambda _: WHOLE, out)),
        scratch_shapes=list(scratch),
        compiler_params=pltpu.CompilerParams(vmem_limit_bytes=64 << 20),
        cost_estimate=pl.CostEstimate(flops=flops, bytes_accessed=0, transcendentals=0),
        name=name,
        **kw,
    )(*ins)


def half_of():
    return lax.axis_index("comp")


def side_of():
    return lax.rem(lax.axis_index("comp") + lax.axis_index("tile"), 2)


def row_at(j, side):
    return jnp.where(side == 0, j, ROWS - 1 - j)


def taker(lines, side, take):
    out = lax.broadcasted_iota(jnp.int32, (lines * 16, 256), 0)
    into = lax.broadcasted_iota(jnp.int32, (lines * 16, 256), 1)
    hit = ((out & 15) == (into >> 4)) & ((into & 15) == take(out >> 4))
    return jnp.where(hit, 1.0, 0.0).astype(BF16)


def open_kernel(state, taps, atm_gain, ocean_gain, head, own_p, *rest):
    sends, keep = rest[: len(SENT)], rest[len(SENT)]
    side = side_of()
    gains = [g[...].astype(F32).reshape(1, HALF) for g in (atm_gain, ocean_gain)]
    own_p[...] = jnp.concatenate([taps[...], *gains, jnp.zeros((5, HALF), F32)], 0)
    high = own_p[...].astype(BF16)
    low = (own_p[...] - high.astype(F32)).astype(BF16)
    head[HALF:, :LANES] = high
    head[HALF:, LANES:] = low
    pick = taker(18, side, lambda n: jnp.where(n < 9, row_at(n, side), row_at(n - 9, 1 - side)))
    for b in range(HALF // 16):
        channels = slice(16 * b, 16 * (b + 1))
        lines = dot(pick, state[channels].reshape(256, COLS)).astype(BF16)
        head[channels, :] = lines[16 * 9 : 16 * 10]
        for j in range(9):
            keep[j, channels, :] = lines[16 * j : 16 * (j + 1)]
            for (first, last), sent in zip(SENT, sends):
                if first <= j < last:
                    sent[j - first, channels, :] = lines[16 * (j + 9) : 16 * (j + 10)]


def params_of(head):
    return head[HALF:, :LANES].astype(F32) + head[HALF:, LANES:].astype(F32)


def gelu(x):
    inner = x * (0.7978845608028654 + 0.035677408136300125 * (x * x))
    return (x * (0.5 + 0.5 * jnp.tanh(inner))).astype(BF16)


def dot(a, b):
    return jnp.dot(a, b, preferred_element_type=F32)


def normed(values, gains):
    total = sum(jnp.sum(v, 0, keepdims=True) for v in values)
    squares = sum(jnp.sum(v * v, 0, keepdims=True) for v in values)
    center = total / CHANNELS
    spread = squares / CHANNELS - center * center
    scale = lax.rsqrt(spread + 1e-06)
    return [((v - center) * scale * g).astype(BF16) for v, g in zip(values, gains)]


def turned_up(up, j, half):
    halves = [up[pl.ds(pl.multiple_of(s * HALF, HALF), HALF), j * 256 : (j + 1) * 256] for s in (half, 1 - half)]
    return jnp.concatenate(halves, 0).T


def turned_down(down, j, half):
    halves = [down[j * 256 : (j + 1) * 256, pl.ds(pl.multiple_of(s * HALF, HALF), HALF)] for s in (half, 1 - half)]
    return jnp.concatenate(halves, 1).T


def ocean_kernel(mine, theirs, own_p, head, keep, up, down, passing, kept, sent, pair, passed, x):
    pair[0] = keep[0]
    pair[1] = head[:HALF, :]
    gains = [own_p[...].T[:, 10:11], params_of(head).T[:, 10:11]]
    own, other = normed([mine[...].astype(F32), theirs[...].astype(F32)], gains)
    x[:HALF, :] = own
    x[HALF:, :] = other
    total = None
    for j in range(2):
        hidden = gelu(dot(turned_up(up, j, half_of()), x[...]))
        part = dot(turned_down(down, j, half_of()), hidden)
        total = part if total is None else total + part
    kept[...] = total[:HALF]
    sent[...] = total[HALF:].astype(BF16)


def start(pairs, sems, at):
    moves = [pltpu.make_async_copy(src, dst, sems.at[at + n]) for n, (src, dst) in enumerate(pairs)]
    for m in moves:
        m.start()
    return moves


def wait(moves):
    for m in moves:
        m.wait()


def mix_kernel(rows, runs_own, runs_other, n_in, leads, *refs):
    refs = list(refs)
    take = lambda n: [refs.pop(0) for _ in range(n)]
    (count,) = take(1) if leads else (None,)
    own_p, head, *weights = take(6 if leads else 3)
    take(0 if leads else 1)
    ocean_ins = take(3) if leads else []
    ins = take(n_in)
    kept, sent = take(2)
    blocks_out, result, slots = take(3) if leads else (None, None, None)
    own_pv, head_pv, own_lines, other_lines, x, blocks, kept_v, sent_v, sems = take(9)
    side = side_of()

    def lines_of(runs, lines):
        for ref, src, n, dst in runs:
            if src is None:
                yield ins[ref].at[pl.ds(0, HALF)], lines.at[dst]
            else:
                yield ins[ref].at[pl.ds(src, n)], lines.at[pl.ds(dst, n)]

    pairs = [(own_p, own_pv), (head.at[pl.ds(HALF, 16)], head_pv)]
    pairs += [*lines_of(runs_own, own_lines), *lines_of(runs_other, other_lines)]
    loads = start(pairs, sems, 0)
    used = len(pairs)
    if leads:
        raw, ocean_v, (result_v, slots_v) = take(4), take(3), take(2)
        ocean_loads = start(list(zip(ocean_ins, ocean_v)), sems, used)
        weight_loads = start(list(zip(weights, raw)), sems, used + 3)
        used += 7
    else:
        weight_loads = start([(weights[0], blocks)], sems, used)
        used += 1
    wait(loads)
    params = []
    for taps in (own_pv[...], head_pv[:, :LANES].astype(F32) + head_pv[:, LANES:].astype(F32)):
        flipped = jnp.concatenate([taps[6:9], taps[3:6], taps[0:3], taps[9:]], 0)
        params.append(jnp.where(side == 0, taps, flipped).T)

    def conv(lines, i, p):
        near = [lines[i + a].astype(F32) for a in range(3)]
        left, middle, right = [
            sum(p[:, 3 * a + b : 3 * a + b + 1] * near[a] for a in range(3)) for b in range(3)
        ]
        return middle + pltpu.roll(left, 1, 1) + pltpu.roll(right, COLS - 1, 1)

    for i in range(rows):
        values = [conv(own_lines, i, params[0]), conv(other_lines, i, params[1])]
        own, other = normed(values, [p[:, 9:10] for p in params])
        x[:HALF, i * COLS : (i + 1) * COLS] = own
        x[HALF:, i * COLS : (i + 1) * COLS] = other
    stores = []
    if leads:
        wait(ocean_loads)
        for s in range(SLOTS):
            cells = slice(s * CELLS_PER_TILE, (s + 1) * CELLS_PER_TILE)
            value = ocean_v[0][:, cells].astype(F32) + (ocean_v[1][:, cells] + ocean_v[2][:, cells].astype(F32))
            value = jnp.where(s < count[0], value, 0.0).astype(BF16)
            result_v[:, cells] = value
            slots_v[s] = value
        stores += start([(result_v, result), (slots_v, slots)], sems, used)
        used += 2
    wait(weight_loads)
    if leads:
        for n, (u, d) in enumerate((raw[:2], raw[2:])):
            for j in range(2):
                blocks[2 * n + j] = turned_up(u, j, half_of())
                blocks[4 + 2 * n + j] = turned_down(d, j, half_of())
        stores += start([(blocks, blocks_out)], sems, used)
        used += 1
    up = blocks[:4].reshape(4 * 256, CHANNELS)
    down = jnp.concatenate([blocks[4 + j] for j in range(4)], 1)
    for i in range(rows):
        hidden = gelu(dot(up, x[:, i * COLS : (i + 1) * COLS]))
        value = dot(down, hidden).astype(BF16)
        kept_v[i] = value[:HALF]
        sent_v[i] = value[HALF:]
        stores += start([(sent_v.at[i], sent.at[i]), (kept_v.at[i], kept.at[i])], sems, used)
        used += 2
    wait(stores)


def regrid_kernel(source, own, swap, e1, e2, swap_e1, swap_e2, w, later, out, table):
    step = pl.program_id(0)
    tile = lax.axis_index("tile")
    core, odd = lax.rem(tile, 2), lax.rem(tile // 2, 2)

    @pl.when(step == 0)
    def _():
        for n, part in enumerate((own, swap, e1, e2, swap_e1, swap_e2)):
            table[n * SLOTS : (n + 1) * SLOTS] = part[...]

    def slab(b, k):
        slot = source[k, b]
        offset = slot // SLOTS - tile
        up = offset > 0
        far = jnp.where(up == (odd == 1), 2, 3)
        part = jnp.where(abs(offset) == 1, jnp.where(up == (core == 0), 1, far + 2), far)
        part = jnp.where(offset == 0, 0, part)
        return table[part * SLOTS + lax.rem(slot, SLOTS)]

    per_step = w.shape[0]
    for n in range(per_step):
        b = step * per_step + n
        slabs = jnp.concatenate([slab(b, 0), slab(b, 1)], 1)
        weight = jnp.concatenate([w[n, 0], w[n, 1]], 1)
        value = lax.dot_general(slabs, weight, (((1,), (1,)), ((), ())), preferred_element_type=F32)
        out[n // 2, :, (n % 2) * 128 : (n % 2 + 1) * 128] = value.astype(BF16)


def final_kernel(n, state, regrid, *rest):
    kept, got, out = rest[:n], rest[n : 2 * n], rest[2 * n]
    side = side_of()
    place = taker(16, side, lambda n: jnp.where(n < 8, row_at(n, side), row_at(n - 8, 1 - side)))
    place = jnp.concatenate([place.T, taker(16, side, lambda n: n).T], 1)
    for b in range(state.shape[0] // 16):
        channels = slice(16 * b, 16 * (b + 1))
        lines = []
        for refs in (kept, got):
            for j in range(ROWS // 2):
                k = [n for n, (p, q) in enumerate(MIXED) if p <= j < q][0]
                lines.append(refs[k][j - MIXED[k][0], channels, :])
        lines += [regrid[r, channels, :] for r in range(ROWS)]
        added = dot(place, jnp.concatenate(lines, 0)).reshape(16, ROWS, COLS)
        out[channels] = (state[channels].astype(F32) + added).astype(BF16)


def on_device(
    atm_state, ocean_state, ocean_count, regrid_src, regrid_w, dw_kernel,
    atm_gain, atm_up, atm_down, ocean_gain, ocean_up, ocean_down,
):
    tiles = lax.axis_size("tile")

    def move(x, to):
        route = []
        for t in range(tiles):
            for c in range(2):
                u, d = to(t, c)
                if 0 <= u < tiles:
                    route.append((t * 2 + c, u * 2 + d))
        return lax.ppermute(x, AXES, route)

    def partner(x):
        return move(x, lambda t, c: (t, 1 - c))

    half_turn = 8 if tiles >= 16 else 0

    def across(x):
        return move(x, lambda t, c: (t ^ half_turn, 1 - c))

    got_up, got_down = across(atm_up), across(atm_down)
    ocean_theirs = partner(ocean_state)
    head_sent, own_p, *sends, keep = call(
        open_kernel,
        [sds((HALF + 16, COLS)), sds((16, HALF), F32)]
        + [sds((b - a, HALF, COLS)) for a, b in SENT]
        + [sds((9, HALF, COLS))],
        (atm_state, dw_kernel, atm_gain, ocean_gain),
        [WHOLE] * 4,
        name="open",
    )
    head = partner(head_sent)
    cells = ocean_state.shape[1]
    ocean_kept, ocean_sent, pair, last_sent = call(
        ocean_kernel,
        [sds((HALF, cells), F32), sds((HALF, cells)), sds((2, HALF, COLS)), sds(sends[-1].shape)],
        (ocean_state, ocean_theirs, own_p, head, keep, ocean_up, ocean_down, sends[-1]),
        [WHOLE] * 7 + [ANY],
        [pltpu.VMEM((256, cells), BF16)],
        out_specs=[WHOLE] * 3 + [ANY],
        input_output_aliases={7: 3},
        name="ocean",
        flops=OCEAN_COST,
    )
    got = [partner(s) for s in (*sends[:-1], last_sent)]
    ocean_got = partner(ocean_sent)
    edges = move(pair, lambda t, c: (t - 1 + 2 * ((t + c) % 2), c))
    kept_rows, got_rows, blocks = [], [], None
    for a, b in MIXED:
        ins, runs_own, runs_other = [keep], [], []
        first = max(a - 1, 0)
        if a == 0:
            runs_own.append((1, 0, 1, 0))
            runs_other += [(1, 1, 1, 0), (2, None, 1, 1)]
            ins += [edges, head]
        runs_own.append((0, first, b + 1 - first, first - a + 1))
        for (p, q), g in zip(SENT, got):
            p, q = max(p, first), min(q, b + 1)
            if p < q:
                runs_other.append((len(ins), p - SENT[[x is g for x in got].index(True)][0], q - p, p - a + 1))
                ins.append(g)
        rows, leads = b - a, blocks is None
        lead_ins = (atm_up, atm_down, got_up, got_down, ocean_state, ocean_kept, ocean_got)
        out = [sds((rows, HALF, COLS))] * 2
        scratch = [
            pltpu.VMEM((16, HALF), F32),
            pltpu.VMEM((16, COLS), BF16),
            pltpu.VMEM((rows + 2, HALF, COLS), BF16),
            pltpu.VMEM((rows + 2, HALF, COLS), BF16),
            pltpu.VMEM((CHANNELS, rows * COLS), BF16),
            pltpu.VMEM((8, 256, 256), BF16),
            pltpu.VMEM((rows, HALF, COLS), BF16),
            pltpu.VMEM((rows, HALF, COLS), BF16),
            pltpu.SemaphoreType.DMA((40,)),
        ]
        if leads:
            out += [sds((8, 256, 256)), sds((HALF, cells)), sds((SLOTS, HALF, CELLS_PER_TILE))]
            scratch += [pltpu.VMEM(w.shape, w.dtype) for w in lead_ins]
            scratch += [pltpu.VMEM((HALF, cells), BF16), pltpu.VMEM((SLOTS, HALF, CELLS_PER_TILE), BF16)]
        args = (ocean_count, own_p, head, *lead_ins, *ins) if leads else (own_p, head, blocks, swapped, *ins)
        kept, sent, *more = call(
            functools.partial(mix_kernel, rows, runs_own, runs_other, len(ins), leads),
            out,
            args,
            ([SMEM] if leads else []) + [ANY] * (len(args) - leads),
            scratch,
            out_specs=[ANY] * len(out),
            name="mix",
        )
        if leads:
            blocks, ocean_result, slots = more
            swapped = move(slots, lambda t, c: (t ^ 1, c))
        kept_rows.append(kept)
        got_rows.append(partner(sent))
    e2 = move(slots, lambda t, c: (t ^ 2, c))
    e1 = move(slots, lambda t, c: (t + 2 if t // 2 % 2 else t - 2, c))
    swap_e1, swap_e2 = [move(e, lambda t, c: (t ^ 1, c)) for e in (e1, e2)]

    steps = 2
    per_step = regrid_src.shape[0] // steps
    table = pl.BlockSpec((SLOTS, HALF, CELLS_PER_TILE), lambda i: (0, 0, 0))
    regrid = call(
        regrid_kernel,
        sds((ROWS, HALF, COLS)),
        (regrid_src.T, slots, swapped, e1, e2, swap_e1, swap_e2, regrid_w, got_rows[0]),
        [SMEM] + [table] * 6 + [pl.BlockSpec((per_step, 2, 128, 128), lambda i: (i, 0, 0, 0)), ANY],
        [pltpu.VMEM((6 * SLOTS, HALF, CELLS_PER_TILE), BF16)],
        grid=(steps,),
        out_specs=pl.BlockSpec((ROWS // steps, HALF, COLS), lambda i: (i, 0, 0)),
        name="regrid",
    )
    depth = HALF // FINAL_STEPS
    rows_spec = [pl.BlockSpec((b - a, depth, COLS), lambda i: (0, i, 0)) for a, b in MIXED]
    state_spec = pl.BlockSpec((depth, ROWS, COLS), lambda i: (i, 0, 0))
    atm_out = call(
        functools.partial(final_kernel, len(MIXED)),
        sds((HALF, ROWS, COLS)),
        (atm_state, regrid, *kept_rows, *got_rows),
        [state_spec, pl.BlockSpec((ROWS, depth, COLS), lambda i: (0, i, 0))] + rows_spec * 2,
        grid=(FINAL_STEPS,),
        out_specs=state_spec,
        name="final",
    )
    return (atm_out, ocean_result)


def solution(mesh):
    return jax.shard_map(
        on_device,
        mesh=mesh,
        in_specs=(
            P("comp", "tile", None),
            P("comp", "tile"),
            P("tile"),
            P("tile", None),
            P("tile", None, None, None),
            P(None, "comp"),
            P("comp"),
            P(None, "comp"),
            P("comp", None),
            P("comp"),
            P(None, "comp"),
            P("comp", None),
        ),
        out_specs=(P("comp", "tile", None), P("comp", "tile")),
        check_vma=False,
    )
```

```python
import functools

import jax
import jax.numpy as jnp
from jax import lax
from jax.experimental import pallas as pl
from jax.experimental.pallas import tpu as pltpu
from jax.sharding import PartitionSpec as P

CHANNELS = 256
HALF = 128
ROWS = 16
COLS = 256
LANES = 128
CELLS_PER_TILE = 128
SLOTS = 4
F32 = jnp.float32
BF16 = jnp.bfloat16
AXES = ("tile", "comp")
WHOLE = pl.BlockSpec()
SMEM = pl.BlockSpec(memory_space=pltpu.SMEM)
ANY = pl.BlockSpec(memory_space=pl.ANY)
FINAL_STEPS = 2
MIX_COST = 30 * 10**9
OCEAN_COST = 8 * 10**9
SENT = ((3, 9), (1, 3))
MIXED = ((4, 8), (0, 4))


def sds(shape, dtype=BF16):
    return jax.ShapeDtypeStruct(shape, dtype)


def call(kernel, out, ins, specs, scratch=(), name=None, flops=0, **kw):
    return pl.pallas_call(
        kernel,
        out_shape=out,
        in_specs=specs,
        out_specs=kw.pop("out_specs", jax.tree.map(lambda _: WHOLE, out)),
        scratch_shapes=list(scratch),
        compiler_params=pltpu.CompilerParams(vmem_limit_bytes=64 << 20),
        cost_estimate=pl.CostEstimate(flops=flops, bytes_accessed=0, transcendentals=0),
        name=name,
        **kw,
    )(*ins)


def half_of():
    return lax.axis_index("comp")


def side_of():
    return lax.rem(lax.axis_index("comp") + lax.axis_index("tile"), 2)


def row_at(j, side):
    return jnp.where(side == 0, j, ROWS - 1 - j)


def taker(lines, side, take):
    out = lax.broadcasted_iota(jnp.int32, (lines * 16, 256), 0)
    into = lax.broadcasted_iota(jnp.int32, (lines * 16, 256), 1)
    hit = ((out & 15) == (into >> 4)) & ((into & 15) == take(out >> 4))
    return jnp.where(hit, 1.0, 0.0).astype(BF16)


def open_kernel(state, taps, atm_gain, ocean_gain, head, own_p, *rest):
    sends, keep = rest[: len(SENT)], rest[len(SENT)]
    side = side_of()
    gains = [g[...].astype(F32).reshape(1, HALF) for g in (atm_gain, ocean_gain)]
    own_p[...] = jnp.concatenate([taps[...], *gains, jnp.zeros((5, HALF), F32)], 0)
    high = own_p[...].astype(BF16)
    low = (own_p[...] - high.astype(F32)).astype(BF16)
    head[HALF:, :LANES] = high
    head[HALF:, LANES:] = low
    pick = taker(18, side, lambda n: jnp.where(n < 9, row_at(n, side), row_at(n - 9, 1 - side)))
    for b in range(HALF // 16):
        channels = slice(16 * b, 16 * (b + 1))
        lines = dot(pick, state[channels].reshape(256, COLS)).astype(BF16)
        head[channels, :] = lines[16 * 9 : 16 * 10]
        for j in range(9):
            keep[j, channels, :] = lines[16 * j : 16 * (j + 1)]
            for (first, last), sent in zip(SENT, sends):
                if first <= j < last:
                    sent[j - first, channels, :] = lines[16 * (j + 9) : 16 * (j + 10)]


def params_of(head):
    return head[HALF:, :LANES].astype(F32) + head[HALF:, LANES:].astype(F32)


def gelu(x):
    x = x.astype(BF16)
    inner = x * (BF16(0.7978845608028654) + BF16(0.035677408136300125) * (x * x))
    return x * (BF16(0.5) + BF16(0.5) * jnp.tanh(inner))


def dot(a, b):
    return jnp.dot(a, b, preferred_element_type=F32)


def normed(values, gains):
    total = sum(jnp.sum(v, 0, keepdims=True) for v in values)
    squares = sum(jnp.sum(v * v, 0, keepdims=True) for v in values)
    center = total / CHANNELS
    spread = squares / CHANNELS - center * center
    scale = lax.rsqrt(spread + 1e-06)
    return [((v - center) * scale * g).astype(BF16) for v, g in zip(values, gains)]


def turned_up(up, j, half):
    halves = [up[pl.ds(pl.multiple_of(s * HALF, HALF), HALF), j * 256 : (j + 1) * 256] for s in (half, 1 - half)]
    return jnp.concatenate(halves, 0).T


def turned_down(down, j, half):
    halves = [down[j * 256 : (j + 1) * 256, pl.ds(pl.multiple_of(s * HALF, HALF), HALF)] for s in (half, 1 - half)]
    return jnp.concatenate(halves, 1).T


def turn_kernel(up, down, own, sent):
    half = half_of()
    for blocks, first in ((own, half), (sent, 1 - half)):
        for j in range(2):
            blocks[j * 256 : (j + 1) * 256] = turned_up(up, j, first)
            blocks[(2 + j) * 256 : (3 + j) * 256] = turned_down(down, j, first)


def ocean_kernel(mine, theirs, own_p, head, keep, up, down, before, kept, sent, pair, x):
    pair[0] = keep[0]
    pair[1] = head[:HALF, :]
    gains = [own_p[...].T[:, 10:11], params_of(head).T[:, 10:11]]
    own, other = normed([mine[...].astype(F32), theirs[...].astype(F32)], gains)
    x[:HALF, :] = own
    x[HALF:, :] = other
    total = None
    for j in range(2):
        hidden = gelu(dot(turned_up(up, j, half_of()), x[...]))
        part = dot(turned_down(down, j, half_of()), hidden)
        total = part if total is None else total + part
    kept[...] = total[:HALF]
    sent[...] = total[HALF:].astype(BF16)


def ocean_result_kernel(count, state, kept, got, passing, result, slots, passed):
    for s in range(SLOTS):
        cells = slice(s * CELLS_PER_TILE, (s + 1) * CELLS_PER_TILE)
        value = state[:, cells].astype(F32) + (kept[:, cells] + got[:, cells].astype(F32))
        value = jnp.where(s < count[0], value, 0.0).astype(BF16)
        result[:, cells] = value
        slots[s] = value


def start(pairs, sems, at):
    moves = [pltpu.make_async_copy(src, dst, sems.at[at + n]) for n, (src, dst) in enumerate(pairs)]
    for m in moves:
        m.start()
    return moves


def wait(moves):
    for m in moves:
        m.wait()


def mix_kernel(rows, runs_own, runs_other, n_in, leads, *refs):
    refs = list(refs)
    take = lambda n: [refs.pop(0) for _ in range(n)]
    own_p, head, *weights = take(4)
    ins = take(n_in)
    take(2 if leads else 0)
    kept, sent = take(2)
    own_pv, head_pv, own_lines, other_lines, x, up, down, kept_v, sent_v, sems = take(10)
    side = side_of()

    def lines_of(runs, lines):
        for ref, src, n, dst in runs:
            if src is None:
                yield ins[ref].at[pl.ds(0, HALF)], lines.at[dst]
            else:
                yield ins[ref].at[pl.ds(src, n)], lines.at[pl.ds(dst, n)]

    pairs = [(own_p, own_pv), (head.at[pl.ds(HALF, 16)], head_pv)]
    pairs += [*lines_of(runs_own, own_lines), *lines_of(runs_other, other_lines)]
    loads = start(pairs, sems, 0)
    used = len(pairs)
    pairs = []
    for n, w in enumerate(weights):
        pairs.append((w.at[pl.ds(0, 512)], up.at[pl.ds(512 * n, 512)]))
        pairs += [
            (w.at[pl.ds(512 + 256 * j, 256)], down.at[:, pl.ds(512 * n + 256 * j, 256)]) for j in range(2)
        ]
    weight_loads = start(pairs, sems, used)
    used += len(pairs)
    wait(loads)
    params = []
    for taps in (own_pv[...], head_pv[:, :LANES].astype(F32) + head_pv[:, LANES:].astype(F32)):
        flipped = jnp.concatenate([taps[6:9], taps[3:6], taps[0:3], taps[9:]], 0)
        params.append(jnp.where(side == 0, taps, flipped).T)

    def conv(lines, i, p):
        near = [lines[i + a].astype(F32) for a in range(3)]
        left, middle, right = [
            sum(p[:, 3 * a + b : 3 * a + b + 1] * near[a] for a in range(3)) for b in range(3)
        ]
        return middle + pltpu.roll(left, 1, 1) + pltpu.roll(right, COLS - 1, 1)

    for i in range(rows):
        values = [conv(own_lines, i, params[0]), conv(other_lines, i, params[1])]
        own, other = normed(values, [p[:, 9:10] for p in params])
        x[:HALF, i * COLS : (i + 1) * COLS] = own
        x[HALF:, i * COLS : (i + 1) * COLS] = other
    stores = []
    wait(weight_loads)
    for i in range(rows):
        hidden = gelu(dot(up[...], x[:, i * COLS : (i + 1) * COLS]))
        value = dot(down[...], hidden).astype(BF16)
        kept_v[i] = value[:HALF]
        sent_v[i] = value[HALF:]
        stores += start([(sent_v.at[i], sent.at[i]), (kept_v.at[i], kept.at[i])], sems, used)
        used += 2
    wait(stores)


def regrid_kernel(source, own, swap, e1, e2, swap_e1, swap_e2, w, later, out, table):
    step = pl.program_id(0)
    tile = lax.axis_index("tile")
    core, odd = lax.rem(tile, 2), lax.rem(tile // 2, 2)

    @pl.when(step == 0)
    def _():
        for n, part in enumerate((own, swap, e1, e2, swap_e1, swap_e2)):
            table[n * SLOTS : (n + 1) * SLOTS] = part[...]

    def slab(b, k):
        slot = source[k, b]
        offset = slot // SLOTS - tile
        up = offset > 0
        far = jnp.where(up == (odd == 1), 2, 3)
        part = jnp.where(abs(offset) == 1, jnp.where(up == (core == 0), 1, far + 2), far)
        part = jnp.where(offset == 0, 0, part)
        return table[part * SLOTS + lax.rem(slot, SLOTS)]

    per_step = w.shape[0]
    for n in range(per_step):
        b = step * per_step + n
        slabs = jnp.concatenate([slab(b, 0), slab(b, 1)], 1)
        weight = jnp.concatenate([w[n, 0], w[n, 1]], 1)
        value = lax.dot_general(slabs, weight, (((1,), (1,)), ((), ())), preferred_element_type=F32)
        out[n // 2, :, (n % 2) * 128 : (n % 2 + 1) * 128] = value.astype(BF16)


def final_kernel(n, state, regrid, *rest):
    kept, got, out = rest[:n], rest[n : 2 * n], rest[2 * n]
    side = side_of()
    place = taker(16, side, lambda n: jnp.where(n < 8, row_at(n, side), row_at(n - 8, 1 - side)))
    place = jnp.concatenate([place.T, taker(16, side, lambda n: n).T], 1)
    for b in range(state.shape[0] // 16):
        channels = slice(16 * b, 16 * (b + 1))
        lines = []
        for refs in (kept, got):
            for j in range(ROWS // 2):
                k = [n for n, (p, q) in enumerate(MIXED) if p <= j < q][0]
                lines.append(refs[k][j - MIXED[k][0], channels, :])
        lines += [regrid[r, channels, :] for r in range(ROWS)]
        added = dot(place, jnp.concatenate(lines, 0)).reshape(16, ROWS, COLS)
        out[channels] = (state[channels].astype(F32) + added).astype(BF16)


def on_device(
    atm_state, ocean_state, ocean_count, regrid_src, regrid_w, dw_kernel,
    atm_gain, atm_up, atm_down, ocean_gain, ocean_up, ocean_down,
):
    tiles = lax.axis_size("tile")

    def move(x, to):
        route = []
        for t in range(tiles):
            for c in range(2):
                u, d = to(t, c)
                if 0 <= u < tiles:
                    route.append((t * 2 + c, u * 2 + d))
        return lax.ppermute(x, AXES, route)

    def partner(x):
        return move(x, lambda t, c: (t, 1 - c))

    half_turn = 8 if tiles >= 16 else 0

    def across(x):
        return move(x, lambda t, c: (t ^ half_turn, 1 - c))

    blocks, blocks_sent = call(
        turn_kernel,
        [sds((1024, 256))] * 2,
        (atm_up, atm_down),
        [WHOLE] * 2,
        name="turn",
    )
    got_blocks = across(blocks_sent)
    ocean_theirs = partner(ocean_state)
    head_sent, own_p, *sends, keep = call(
        open_kernel,
        [sds((HALF + 16, COLS)), sds((16, HALF), F32)]
        + [sds((b - a, HALF, COLS)) for a, b in SENT]
        + [sds((9, HALF, COLS))],
        (atm_state, dw_kernel, atm_gain, ocean_gain),
        [WHOLE] * 4,
        name="open",
    )
    head = partner(head_sent)
    cells = ocean_state.shape[1]
    ocean_kept, ocean_sent, pair = call(
        ocean_kernel,
        [sds((HALF, cells), F32), sds((HALF, cells)), sds((2, HALF, COLS))],
        (ocean_state, ocean_theirs, own_p, head, keep, ocean_up, ocean_down, blocks),
        [WHOLE] * 7 + [ANY],
        [pltpu.VMEM((256, cells), BF16)],
        out_specs=[WHOLE] * 3,
        name="ocean",
        flops=OCEAN_COST,
    )
    ocean_got = partner(ocean_sent)
    edges = move(pair, lambda t, c: (t - 1 + 2 * ((t + c) % 2), c))
    ocean_result, slots, last_sent = call(
        ocean_result_kernel,
        [sds((HALF, cells)), sds((SLOTS, HALF, CELLS_PER_TILE)), sds(sends[-1].shape)],
        (ocean_count, ocean_state, ocean_kept, ocean_got, sends[-1]),
        [SMEM, WHOLE, WHOLE, WHOLE, ANY],
        out_specs=[WHOLE, WHOLE, ANY],
        input_output_aliases={4: 2},
        name="result",
    )
    got = [partner(s) for s in (*sends[:-1], last_sent)]
    swapped = move(slots, lambda t, c: (t ^ 1, c))
    kept_rows, got_rows = [], []
    for a, b in MIXED:
        ins, runs_own, runs_other = [keep], [], []
        first = max(a - 1, 0)
        if a == 0:
            runs_own.append((1, 0, 1, 0))
            runs_other += [(1, 1, 1, 0), (2, None, 1, 1)]
            ins += [edges, head]
        runs_own.append((0, first, b + 1 - first, first - a + 1))
        for (p, q), g in zip(SENT, got):
            p, q = max(p, first), min(q, b + 1)
            if p < q:
                runs_other.append((len(ins), p - SENT[[x is g for x in got].index(True)][0], q - p, p - a + 1))
                ins.append(g)
        rows, leads = b - a, not kept_rows
        out = [sds((rows, HALF, COLS))] * 2
        scratch = [
            pltpu.VMEM((16, HALF), F32),
            pltpu.VMEM((16, COLS), BF16),
            pltpu.VMEM((rows + 2, HALF, COLS), BF16),
            pltpu.VMEM((rows + 2, HALF, COLS), BF16),
            pltpu.VMEM((CHANNELS, rows * COLS), BF16),
            pltpu.VMEM((1024, 256), BF16),
            pltpu.VMEM((256, 1024), BF16),
            pltpu.VMEM((rows, HALF, COLS), BF16),
            pltpu.VMEM((rows, HALF, COLS), BF16),
            pltpu.SemaphoreType.DMA((40,)),
        ]
        args = (own_p, head, blocks, got_blocks, *ins, *((edges, got[-1]) if leads else ()))
        kept, sent = call(
            functools.partial(mix_kernel, rows, runs_own, runs_other, len(ins), leads),
            out,
            args,
            [ANY] * len(args),
            scratch,
            out_specs=[ANY] * len(out),
            name="mix",
            flops=MIX_COST if leads else 0,
        )
        kept_rows.append(kept)
        got_rows.append(partner(sent))
    e2 = move(slots, lambda t, c: (t ^ 2, c))
    e1 = move(slots, lambda t, c: (t + 2 if t // 2 % 2 else t - 2, c))
    swap_e1, swap_e2 = [move(e, lambda t, c: (t ^ 1, c)) for e in (e1, e2)]

    steps = 2
    per_step = regrid_src.shape[0] // steps
    table = pl.BlockSpec((SLOTS, HALF, CELLS_PER_TILE), lambda i: (0, 0, 0))
    regrid = call(
        regrid_kernel,
        sds((ROWS, HALF, COLS)),
        (regrid_src.T, slots, swapped, e1, e2, swap_e1, swap_e2, regrid_w, got_rows[0]),
        [SMEM] + [table] * 6 + [pl.BlockSpec((per_step, 2, 128, 128), lambda i: (i, 0, 0, 0)), ANY],
        [pltpu.VMEM((6 * SLOTS, HALF, CELLS_PER_TILE), BF16)],
        grid=(steps,),
        out_specs=pl.BlockSpec((ROWS // steps, HALF, COLS), lambda i: (i, 0, 0)),
        name="regrid",
    )
    depth = HALF // FINAL_STEPS
    rows_spec = [pl.BlockSpec((b - a, depth, COLS), lambda i: (0, i, 0)) for a, b in MIXED]
    state_spec = pl.BlockSpec((depth, ROWS, COLS), lambda i: (i, 0, 0))
    atm_out = call(
        functools.partial(final_kernel, len(MIXED)),
        sds((HALF, ROWS, COLS)),
        (atm_state, regrid, *kept_rows, *got_rows),
        [state_spec, pl.BlockSpec((ROWS, depth, COLS), lambda i: (0, i, 0))] + rows_spec * 2,
        grid=(FINAL_STEPS,),
        out_specs=state_spec,
        name="final",
    )
    return (atm_out, ocean_result)


def solution(mesh):
    return jax.shard_map(
        on_device,
        mesh=mesh,
        in_specs=(
            P("comp", "tile", None),
            P("comp", "tile"),
            P("tile"),
            P("tile", None),
            P("tile", None, None, None),
            P(None, "comp"),
            P("comp"),
            P(None, "comp"),
            P("comp", None),
            P("comp"),
            P(None, "comp"),
            P("comp", None),
        ),
        out_specs=(P("comp", "tile", None), P("comp", "tile")),
        check_vma=False,
    )
```

```python
import functools

import jax
import jax.numpy as jnp
from jax import lax
from jax.experimental import pallas as pl
from jax.experimental.pallas import tpu as pltpu
from jax.sharding import PartitionSpec as P

CHANNELS = 256
HALF = 128
ROWS = 16
COLS = 256
LANES = 128
CELLS_PER_TILE = 128
SLOTS = 4
F32 = jnp.float32
BF16 = jnp.bfloat16
AXES = ("tile", "comp")
WHOLE = pl.BlockSpec()
SMEM = pl.BlockSpec(memory_space=pltpu.SMEM)
ANY = pl.BlockSpec(memory_space=pl.ANY)
FINAL_STEPS = 2
MIX_COST = 30 * 10**9
OCEAN_COST = 8 * 10**9
SENT = ((3, 9), (1, 3))
MIXED = ((4, 8), (0, 4))


def sds(shape, dtype=BF16):
    return jax.ShapeDtypeStruct(shape, dtype)


def call(kernel, out, ins, specs, scratch=(), name=None, flops=0, **kw):
    return pl.pallas_call(
        kernel,
        out_shape=out,
        in_specs=specs,
        out_specs=kw.pop("out_specs", jax.tree.map(lambda _: WHOLE, out)),
        scratch_shapes=list(scratch),
        compiler_params=pltpu.CompilerParams(vmem_limit_bytes=40 << 20),
        cost_estimate=pl.CostEstimate(flops=flops, bytes_accessed=0, transcendentals=0),
        name=name,
        **kw,
    )(*ins)


def start(pairs, sems, at):
    moves = [pltpu.make_async_copy(src, dst, sems.at[at + n]) for n, (src, dst) in enumerate(pairs)]
    for m in moves:
        m.start()
    return moves


def wait(moves):
    for m in moves:
        m.wait()


def half_of():
    return lax.axis_index("comp")


def side_of():
    return lax.rem(lax.axis_index("comp") + lax.axis_index("tile"), 2)


def row_at(j, side):
    return jnp.where(side == 0, j, ROWS - 1 - j)


def taker(lines, side, take):
    out = lax.broadcasted_iota(jnp.int32, (lines * 16, 256), 0)
    into = lax.broadcasted_iota(jnp.int32, (lines * 16, 256), 1)
    hit = ((out & 15) == (into >> 4)) & ((into & 15) == take(out >> 4))
    return jnp.where(hit, 1.0, 0.0).astype(BF16)


def open_kernel(state_in, taps_in, atm_gain_in, ocean_gain_in, head, own_p, *rest):
    sends, (keep, state, taps, atm_gain, ocean_gain, sems) = rest[: len(SENT)], rest[len(SENT) :]
    pairs = [(taps_in, taps), (atm_gain_in, atm_gain), (ocean_gain_in, ocean_gain)]
    pieces = [pl.ds(64 * n, 64) for n in range(2)]
    pairs += [(state_in.at[p], state.at[p]) for p in pieces]
    loads = start(pairs, sems, 0)
    wait(loads[:3])
    side = side_of()
    gains = [g[...].astype(F32).reshape(1, HALF) for g in (atm_gain, ocean_gain)]
    own_p[...] = jnp.concatenate([taps[...], *gains, jnp.zeros((5, HALF), F32)], 0)
    high = own_p[...].astype(BF16)
    low = (own_p[...] - high.astype(F32)).astype(BF16)
    head[HALF:, :LANES] = high
    head[HALF:, LANES:] = low
    pick = taker(18, side, lambda n: jnp.where(n < 9, row_at(n, side), row_at(n - 9, 1 - side)))
    for b in range(HALF // 16):
        if b % 4 == 0:
            loads[3 + b // 4].wait()
        channels = slice(16 * b, 16 * (b + 1))
        lines = dot(pick, state[channels].reshape(256, COLS)).astype(BF16)
        head[channels, :] = lines[16 * 9 : 16 * 10]
        for j in range(9):
            keep[j, channels, :] = lines[16 * j : 16 * (j + 1)]
            for (first, last), sent in zip(SENT, sends):
                if first <= j < last:
                    sent[j - first, channels, :] = lines[16 * (j + 9) : 16 * (j + 10)]


def params_of(head):
    return head[HALF:, :LANES].astype(F32) + head[HALF:, LANES:].astype(F32)


def gelu(x):
    x = x.astype(BF16)
    inner = x * (BF16(0.7978845608028654) + BF16(0.035677408136300125) * (x * x))
    return x * (BF16(0.5) + BF16(0.5) * jnp.tanh(inner))


def dot(a, b):
    return jnp.dot(a, b, preferred_element_type=F32)


def normed(values, gains):
    total = sum(jnp.sum(v, 0, keepdims=True) for v in values)
    squares = sum(jnp.sum(v * v, 0, keepdims=True) for v in values)
    center = total / CHANNELS
    spread = squares / CHANNELS - center * center
    scale = lax.rsqrt(spread + 1e-06)
    return [((v - center) * scale * g).astype(BF16) for v, g in zip(values, gains)]


def turned_up(up, j, half):
    halves = [up[pl.ds(pl.multiple_of(s * HALF, HALF), HALF), j * 256 : (j + 1) * 256] for s in (half, 1 - half)]
    return jnp.concatenate(halves, 0).T


def turned_down(down, j, half):
    halves = [down[j * 256 : (j + 1) * 256, pl.ds(pl.multiple_of(s * HALF, HALF), HALF)] for s in (half, 1 - half)]
    return jnp.concatenate(halves, 1).T


def turn_kernel(up_in, down_in, own, sent, up, down, sems):
    wait(start([(up_in, up), (down_in, down)], sems, 0))
    half = half_of()
    for blocks, first in ((own, half), (sent, 1 - half)):
        for j in range(2):
            blocks[j * 256 : (j + 1) * 256] = turned_up(up, j, first)
            blocks[(2 + j) * 256 : (3 + j) * 256] = turned_down(down, j, first)


def ocean_kernel(
    mine_in, theirs, own_p, head, keep, up_in, down_in, before, kept, sent, pair, x, mine, up, down, sems
):
    loads = start([(mine_in, mine), (up_in, up), (down_in, down)], sems, 0)
    pair[0] = keep[0]
    pair[1] = head[:HALF, :]
    gains = [own_p[...].T[:, 10:11], params_of(head).T[:, 10:11]]
    wait(loads)
    own, other = normed([mine[...].astype(F32), theirs[...].astype(F32)], gains)
    x[:HALF, :] = own
    x[HALF:, :] = other
    total = None
    for j in range(2):
        hidden = gelu(dot(turned_up(up, j, half_of()), x[...]))
        part = dot(turned_down(down, j, half_of()), hidden)
        total = part if total is None else total + part
    kept[...] = total[:HALF]
    sent[...] = total[HALF:].astype(BF16)


def ocean_result_kernel(count, state, kept, got, passing, result, slots, passed):
    for s in range(SLOTS):
        cells = slice(s * CELLS_PER_TILE, (s + 1) * CELLS_PER_TILE)
        value = state[:, cells].astype(F32) + (kept[:, cells] + got[:, cells].astype(F32))
        value = jnp.where(s < count[0], value, 0.0).astype(BF16)
        result[:, cells] = value
        slots[s] = value


def mix_kernel(rows, own_lines, other_lines, n_in, n_order, own_p, head, own_w, got_w, *refs):
    ins, (kept, sent, x) = refs[:n_in], refs[n_in + n_order :]
    side = side_of()
    params = []
    for taps in (own_p[...], params_of(head)):
        flipped = jnp.concatenate([taps[6:9], taps[3:6], taps[0:3], taps[9:]], 0)
        params.append(jnp.where(side == 0, taps, flipped).T)

    def line(place):
        ref, index = place
        return (ins[ref][:HALF, :] if index is None else ins[ref][index]).astype(F32)

    def conv(places, p):
        near = [line(place) for place in places]
        left, middle, right = [
            sum(p[:, 3 * a + b : 3 * a + b + 1] * near[a] for a in range(3)) for b in range(3)
        ]
        return middle + pltpu.roll(left, 1, 1) + pltpu.roll(right, COLS - 1, 1)

    for i in range(rows):
        values = [conv(own_lines[i : i + 3], params[0]), conv(other_lines[i : i + 3], params[1])]
        own, other = normed(values, [p[:, 9:10] for p in params])
        x[:HALF, i * COLS : (i + 1) * COLS] = own
        x[HALF:, i * COLS : (i + 1) * COLS] = other
    up = jnp.concatenate([own_w[:512], got_w[:512]], 0)
    down = jnp.concatenate([w[512 + 256 * j : 768 + 256 * j] for w in (own_w, got_w) for j in range(2)], 1)
    for i in range(rows):
        hidden = gelu(dot(up, x[:, i * COLS : (i + 1) * COLS]))
        value = dot(down, hidden).astype(BF16)
        kept[i] = value[:HALF]
        sent[i] = value[HALF:]


def regrid_kernel(source, own, swap, e1, e2, swap_e1, swap_e2, w, later, out, table):
    step = pl.program_id(0)
    tile = lax.axis_index("tile")
    core, odd = lax.rem(tile, 2), lax.rem(tile // 2, 2)

    @pl.when(step == 0)
    def _():
        for n, part in enumerate((own, swap, e1, e2, swap_e1, swap_e2)):
            table[n * SLOTS : (n + 1) * SLOTS] = part[...]

    def slab(b, k):
        slot = source[k, b]
        offset = slot // SLOTS - tile
        up = offset > 0
        far = jnp.where(up == (odd == 1), 2, 3)
        part = jnp.where(abs(offset) == 1, jnp.where(up == (core == 0), 1, far + 2), far)
        part = jnp.where(offset == 0, 0, part)
        return table[part * SLOTS + lax.rem(slot, SLOTS)]

    per_step = w.shape[0]
    for n in range(per_step):
        b = step * per_step + n
        slabs = jnp.concatenate([slab(b, 0), slab(b, 1)], 1)
        weight = jnp.concatenate([w[n, 0], w[n, 1]], 1)
        value = lax.dot_general(slabs, weight, (((1,), (1,)), ((), ())), preferred_element_type=F32)
        out[n // 2, :, (n % 2) * 128 : (n % 2 + 1) * 128] = value.astype(BF16)


def final_kernel(n, state, regrid, *rest):
    kept, got, out = rest[:n], rest[n : 2 * n], rest[2 * n]
    side = side_of()
    place = taker(16, side, lambda n: jnp.where(n < 8, row_at(n, side), row_at(n - 8, 1 - side)))
    place = jnp.concatenate([place.T, taker(16, side, lambda n: n).T], 1)
    for b in range(state.shape[0] // 16):
        channels = slice(16 * b, 16 * (b + 1))
        lines = []
        for refs in (kept, got):
            for j in range(ROWS // 2):
                k = [n for n, (p, q) in enumerate(MIXED) if p <= j < q][0]
                lines.append(refs[k][j - MIXED[k][0], channels, :])
        lines += [regrid[r, channels, :] for r in range(ROWS)]
        added = dot(place, jnp.concatenate(lines, 0)).reshape(16, ROWS, COLS)
        out[channels] = (state[channels].astype(F32) + added).astype(BF16)


def on_device(
    atm_state, ocean_state, ocean_count, regrid_src, regrid_w, dw_kernel,
    atm_gain, atm_up, atm_down, ocean_gain, ocean_up, ocean_down,
):
    tiles = lax.axis_size("tile")

    def move(x, to):
        route = []
        for t in range(tiles):
            for c in range(2):
                u, d = to(t, c)
                if 0 <= u < tiles:
                    route.append((t * 2 + c, u * 2 + d))
        return lax.ppermute(x, AXES, route)

    def partner(x):
        return move(x, lambda t, c: (t, 1 - c))

    half_turn = 8 if tiles >= 16 else 0

    def across(x):
        return move(x, lambda t, c: (t ^ half_turn, 1 - c))

    blocks, blocks_sent = call(
        turn_kernel,
        [sds((1024, 256))] * 2,
        (atm_up, atm_down),
        [ANY] * 2,
        [pltpu.VMEM(v.shape, v.dtype) for v in (atm_up, atm_down)] + [pltpu.SemaphoreType.DMA((2,))],
        name="turn",
    )
    got_blocks = across(blocks_sent)
    ocean_theirs = partner(ocean_state)
    head_sent, own_p, *sends, keep = call(
        open_kernel,
        [sds((HALF + 16, COLS)), sds((16, HALF), F32)]
        + [sds((b - a, HALF, COLS)) for a, b in SENT]
        + [sds((9, HALF, COLS))],
        (atm_state, dw_kernel, atm_gain, ocean_gain),
        [ANY] * 4,
        [pltpu.VMEM(v.shape, v.dtype) for v in (atm_state, dw_kernel, atm_gain, ocean_gain)]
        + [pltpu.SemaphoreType.DMA((5,))],
        name="open",
    )
    head = partner(head_sent)
    cells = ocean_state.shape[1]
    ocean_kept, ocean_sent, pair = call(
        ocean_kernel,
        [sds((HALF, cells), F32), sds((HALF, cells)), sds((2, HALF, COLS))],
        (ocean_state, ocean_theirs, own_p, head, keep, ocean_up, ocean_down, blocks),
        [ANY] + [WHOLE] * 4 + [ANY] * 3,
        [pltpu.VMEM((256, cells), BF16)]
        + [pltpu.VMEM(v.shape, v.dtype) for v in (ocean_state, ocean_up, ocean_down)]
        + [pltpu.SemaphoreType.DMA((3,))],
        out_specs=[WHOLE] * 3,
        name="ocean",
        flops=OCEAN_COST,
    )
    ocean_got = partner(ocean_sent)
    edges = move(pair, lambda t, c: (t - 1 + 2 * ((t + c) % 2), c))
    ocean_result, slots, last_sent = call(
        ocean_result_kernel,
        [sds((HALF, cells)), sds((SLOTS, HALF, CELLS_PER_TILE)), sds(sends[-1].shape)],
        (ocean_count, ocean_state, ocean_kept, ocean_got, sends[-1]),
        [SMEM, WHOLE, WHOLE, WHOLE, ANY],
        out_specs=[WHOLE, WHOLE, ANY],
        input_output_aliases={4: 2},
        name="result",
    )
    got = [partner(s) for s in (*sends[:-1], last_sent)]
    swapped = move(slots, lambda t, c: (t ^ 1, c))
    kept_rows, got_rows = [], []
    for a, b in MIXED:
        ins, own_lines, other_lines = [keep], [], []
        for j in range(a - 1, b + 1):
            if j < 0:
                own_lines.append((len(ins), 0))
                other_lines.append((len(ins), 1))
                ins.append(edges)
                continue
            own_lines.append((0, j))
            if j == 0:
                other_lines.append((len(ins), None))
                ins.append(head)
                continue
            k = [n for n, (p, q) in enumerate(SENT) if p <= j < q][0]
            place = [n for n, x in enumerate(ins) if x is got[k]] or [len(ins)]
            ins += [got[k]] * (place[0] == len(ins))
            other_lines.append((place[0], j - SENT[k][0]))
        rows, leads = b - a, not kept_rows
        order = (edges, got[-1]) if leads else ()
        kept, sent = call(
            functools.partial(mix_kernel, rows, own_lines, other_lines, len(ins), len(order)),
            [sds((rows, HALF, COLS))] * 2,
            (own_p, head, blocks, got_blocks, *ins, *order),
            [WHOLE] * (4 + len(ins)) + [ANY] * len(order),
            [pltpu.VMEM((CHANNELS, rows * COLS), BF16)],
            name="mix",
            flops=MIX_COST if leads else 0,
        )
        kept_rows.append(kept)
        got_rows.append(partner(sent))
    e2 = move(slots, lambda t, c: (t ^ 2, c))
    e1 = move(slots, lambda t, c: (t + 2 if t // 2 % 2 else t - 2, c))
    swap_e1, swap_e2 = [move(e, lambda t, c: (t ^ 1, c)) for e in (e1, e2)]

    steps = 2
    per_step = regrid_src.shape[0] // steps
    table = pl.BlockSpec((SLOTS, HALF, CELLS_PER_TILE), lambda i: (0, 0, 0))
    regrid = call(
        regrid_kernel,
        sds((ROWS, HALF, COLS)),
        (regrid_src.T, slots, swapped, e1, e2, swap_e1, swap_e2, regrid_w, got_rows[0]),
        [SMEM] + [table] * 6 + [pl.BlockSpec((per_step, 2, 128, 128), lambda i: (i, 0, 0, 0)), ANY],
        [pltpu.VMEM((6 * SLOTS, HALF, CELLS_PER_TILE), BF16)],
        grid=(steps,),
        out_specs=pl.BlockSpec((ROWS // steps, HALF, COLS), lambda i: (i, 0, 0)),
        name="regrid",
    )
    depth = HALF // FINAL_STEPS
    rows_spec = [pl.BlockSpec((b - a, depth, COLS), lambda i: (0, i, 0)) for a, b in MIXED]
    state_spec = pl.BlockSpec((depth, ROWS, COLS), lambda i: (i, 0, 0))
    atm_out = call(
        functools.partial(final_kernel, len(MIXED)),
        sds((HALF, ROWS, COLS)),
        (atm_state, regrid, *kept_rows, *got_rows),
        [state_spec, pl.BlockSpec((ROWS, depth, COLS), lambda i: (0, i, 0))] + rows_spec * 2,
        grid=(FINAL_STEPS,),
        out_specs=state_spec,
        name="final",
    )
    return (atm_out, ocean_result)


def solution(mesh):
    return jax.shard_map(
        on_device,
        mesh=mesh,
        in_specs=(
            P("comp", "tile", None),
            P("comp", "tile"),
            P("tile"),
            P("tile", None),
            P("tile", None, None, None),
            P(None, "comp"),
            P("comp"),
            P(None, "comp"),
            P("comp", None),
            P("comp"),
            P(None, "comp"),
            P("comp", None),
        ),
        out_specs=(P("comp", "tile", None), P("comp", "tile")),
        check_vma=False,
    )
```

```python
import functools

import jax
import jax.numpy as jnp
from jax import lax
from jax.experimental import pallas as pl
from jax.experimental.pallas import tpu as pltpu
from jax.sharding import PartitionSpec as P

CHANNELS = 256
HALF = 128
ROWS = 16
COLS = 256
LANES = 128
CELLS_PER_TILE = 128
SLOTS = 4
F32 = jnp.float32
BF16 = jnp.bfloat16
AXES = ("tile", "comp")
WHOLE = pl.BlockSpec()
SMEM = pl.BlockSpec(memory_space=pltpu.SMEM)
ANY = pl.BlockSpec(memory_space=pl.ANY)
FINAL_STEPS = 2
MIX_COST = 30 * 10**9
OCEAN_COST = 8 * 10**9
SENT = ((3, 9), (1, 3))
MIXED = ((4, 8), (0, 4))


def sds(shape, dtype=BF16):
    return jax.ShapeDtypeStruct(shape, dtype)


def call(kernel, out, ins, specs, scratch=(), name=None, flops=0, **kw):
    return pl.pallas_call(
        kernel,
        out_shape=out,
        in_specs=specs,
        out_specs=kw.pop("out_specs", jax.tree.map(lambda _: WHOLE, out)),
        scratch_shapes=list(scratch),
        compiler_params=pltpu.CompilerParams(vmem_limit_bytes=40 << 20),
        cost_estimate=pl.CostEstimate(flops=flops, bytes_accessed=0, transcendentals=0),
        name=name,
        **kw,
    )(*ins)


def start(pairs, sems, at):
    moves = [pltpu.make_async_copy(src, dst, sems.at[at + n]) for n, (src, dst) in enumerate(pairs)]
    for m in moves:
        m.start()
    return moves


def wait(moves):
    for m in moves:
        m.wait()


def half_of():
    return lax.axis_index("comp")


def side_of():
    return lax.rem(lax.axis_index("comp") + lax.axis_index("tile"), 2)


def row_at(j, side):
    return jnp.where(side == 0, j, ROWS - 1 - j)


def taker(lines, side, take):
    out = lax.broadcasted_iota(jnp.int32, (lines * 16, 256), 0)
    into = lax.broadcasted_iota(jnp.int32, (lines * 16, 256), 1)
    hit = ((out & 15) == (into >> 4)) & ((into & 15) == take(out >> 4))
    return jnp.where(hit, 1.0, 0.0).astype(BF16)


def open_kernel(state_in, taps_in, atm_gain_in, ocean_gain_in, head, own_p, *rest):
    sends, (keep, state, taps, atm_gain, ocean_gain, sems) = rest[: len(SENT)], rest[len(SENT) :]
    pairs = [(taps_in, taps), (atm_gain_in, atm_gain), (ocean_gain_in, ocean_gain)]
    pieces = [pl.ds(64 * n, 64) for n in range(2)]
    pairs += [(state_in.at[p], state.at[p]) for p in pieces]
    loads = start(pairs, sems, 0)
    wait(loads[:3])
    side = side_of()
    gains = [g[...].astype(F32).reshape(1, HALF) for g in (atm_gain, ocean_gain)]
    own_p[...] = jnp.concatenate([taps[...], *gains, jnp.zeros((5, HALF), F32)], 0)
    high = own_p[...].astype(BF16)
    low = (own_p[...] - high.astype(F32)).astype(BF16)
    head[HALF:, :LANES] = high
    head[HALF:, LANES:] = low
    pick = taker(18, side, lambda n: jnp.where(n < 9, row_at(n, side), row_at(n - 9, 1 - side)))
    for b in range(HALF // 16):
        if b % 4 == 0:
            loads[3 + b // 4].wait()
        channels = slice(16 * b, 16 * (b + 1))
        lines = dot(pick, state[channels].reshape(256, COLS)).astype(BF16)
        head[channels, :] = lines[16 * 9 : 16 * 10]
        for j in range(9):
            keep[j, channels, :] = lines[16 * j : 16 * (j + 1)]
            for (first, last), sent in zip(SENT, sends):
                if first <= j < last:
                    sent[j - first, channels, :] = lines[16 * (j + 9) : 16 * (j + 10)]


def params_of(head):
    return head[HALF:, :LANES].astype(F32) + head[HALF:, LANES:].astype(F32)


def gelu(x):
    x = x.astype(BF16)
    inner = x * (BF16(0.7978845608028654) + BF16(0.035677408136300125) * (x * x))
    return x * (BF16(0.5) + BF16(0.5) * jnp.tanh(inner))


def dot(a, b):
    return jnp.dot(a, b, preferred_element_type=F32)


def normed(values, gains):
    total = sum(jnp.sum(v, 0, keepdims=True) for v in values)
    squares = sum(jnp.sum(v * v, 0, keepdims=True) for v in values)
    center = total / CHANNELS
    spread = squares / CHANNELS - center * center
    scale = lax.rsqrt(spread + 1e-06)
    return [((v - center) * scale * g).astype(BF16) for v, g in zip(values, gains)]


def turned_up(up, j, half):
    halves = [up[pl.ds(pl.multiple_of(s * HALF, HALF), HALF), j * 256 : (j + 1) * 256] for s in (half, 1 - half)]
    return jnp.concatenate(halves, 0).T


def turned_down(down, j, half):
    halves = [down[j * 256 : (j + 1) * 256, pl.ds(pl.multiple_of(s * HALF, HALF), HALF)] for s in (half, 1 - half)]
    return jnp.concatenate(halves, 1).T


def turn_kernel(up_in, down_in, own, sent, up, down, sems):
    wait(start([(up_in, up), (down_in, down)], sems, 0))
    half = half_of()
    for blocks, first in ((own, half), (sent, 1 - half)):
        for j in range(2):
            blocks[j * 256 : (j + 1) * 256] = turned_up(up, j, first)
            blocks[(2 + j) * 256 : (3 + j) * 256] = turned_down(down, j, first)


def ocean_kernel(
    mine_in, theirs, own_p, head, keep, up_in, down_in, before, passing, kept, sent, pair, passed, x, mine, up, down, sems
):
    loads = start([(mine_in, mine), (up_in, up), (down_in, down)], sems, 0)
    pair[0] = keep[0]
    pair[1] = head[:HALF, :]
    gains = [own_p[...].T[:, 10:11], params_of(head).T[:, 10:11]]
    wait(loads)
    own, other = normed([mine[...].astype(F32), theirs[...].astype(F32)], gains)
    x[:HALF, :] = own
    x[HALF:, :] = other
    total = None
    for j in range(2):
        hidden = gelu(dot(turned_up(up, j, half_of()), x[...]))
        part = dot(turned_down(down, j, half_of()), hidden)
        total = part if total is None else total + part
    kept[...] = total[:HALF]
    sent[...] = total[HALF:].astype(BF16)


def ocean_result_kernel(count, state, kept, got, result, slots):
    for s in range(SLOTS):
        cells = slice(s * CELLS_PER_TILE, (s + 1) * CELLS_PER_TILE)
        value = state[:, cells].astype(F32) + (kept[:, cells] + got[:, cells].astype(F32))
        value = jnp.where(s < count[0], value, 0.0).astype(BF16)
        result[:, cells] = value
        slots[s] = value


def mix_kernel(rows, own_lines, other_lines, n_in, n_order, own_p, head, own_w, got_w, *refs):
    ins, (kept, sent, x) = refs[:n_in], refs[n_in + n_order :]
    side = side_of()
    params = []
    for taps in (own_p[...], params_of(head)):
        flipped = jnp.concatenate([taps[6:9], taps[3:6], taps[0:3], taps[9:]], 0)
        params.append(jnp.where(side == 0, taps, flipped).T)

    def line(place):
        ref, index = place
        return (ins[ref][:HALF, :] if index is None else ins[ref][index]).astype(F32)

    def conv(places, p):
        near = [line(place) for place in places]
        left, middle, right = [
            sum(p[:, 3 * a + b : 3 * a + b + 1] * near[a] for a in range(3)) for b in range(3)
        ]
        return middle + pltpu.roll(left, 1, 1) + pltpu.roll(right, COLS - 1, 1)

    for i in range(rows):
        values = [conv(own_lines[i : i + 3], params[0]), conv(other_lines[i : i + 3], params[1])]
        own, other = normed(values, [p[:, 9:10] for p in params])
        x[:HALF, i * COLS : (i + 1) * COLS] = own
        x[HALF:, i * COLS : (i + 1) * COLS] = other
    up = jnp.concatenate([own_w[:512], got_w[:512]], 0)
    down = jnp.concatenate([w[512 + 256 * j : 768 + 256 * j] for w in (own_w, got_w) for j in range(2)], 1)
    for i in range(rows):
        hidden = gelu(dot(up, x[:, i * COLS : (i + 1) * COLS]))
        value = dot(down, hidden).astype(BF16)
        kept[i] = value[:HALF]
        sent[i] = value[HALF:]


def regrid_kernel(source, own, swap, e1, e2, swap_e1, swap_e2, w, later, out, table):
    step = pl.program_id(0)
    tile = lax.axis_index("tile")
    core, odd = lax.rem(tile, 2), lax.rem(tile // 2, 2)

    @pl.when(step == 0)
    def _():
        for n, part in enumerate((own, swap, e1, e2, swap_e1, swap_e2)):
            table[n * SLOTS : (n + 1) * SLOTS] = part[...]

    def slab(b, k):
        slot = source[k, b]
        offset = slot // SLOTS - tile
        up = offset > 0
        far = jnp.where(up == (odd == 1), 2, 3)
        part = jnp.where(abs(offset) == 1, jnp.where(up == (core == 0), 1, far + 2), far)
        part = jnp.where(offset == 0, 0, part)
        return table[part * SLOTS + lax.rem(slot, SLOTS)]

    per_step = w.shape[0]
    for n in range(per_step):
        b = step * per_step + n
        slabs = jnp.concatenate([slab(b, 0), slab(b, 1)], 1)
        weight = jnp.concatenate([w[n, 0], w[n, 1]], 1)
        value = lax.dot_general(slabs, weight, (((1,), (1,)), ((), ())), preferred_element_type=F32)
        out[n // 2, :, (n % 2) * 128 : (n % 2 + 1) * 128] = value.astype(BF16)


def final_kernel(n, state, regrid, *rest):
    kept, got, out = rest[:n], rest[n : 2 * n], rest[2 * n]
    side = side_of()
    place = taker(16, side, lambda n: jnp.where(n < 8, row_at(n, side), row_at(n - 8, 1 - side)))
    place = jnp.concatenate([place.T, taker(16, side, lambda n: n).T], 1)
    for b in range(state.shape[0] // 16):
        channels = slice(16 * b, 16 * (b + 1))
        lines = []
        for refs in (kept, got):
            for j in range(ROWS // 2):
                k = [n for n, (p, q) in enumerate(MIXED) if p <= j < q][0]
                lines.append(refs[k][j - MIXED[k][0], channels, :])
        lines += [regrid[r, channels, :] for r in range(ROWS)]
        added = dot(place, jnp.concatenate(lines, 0)).reshape(16, ROWS, COLS)
        out[channels] = (state[channels].astype(F32) + added).astype(BF16)


def on_device(
    atm_state, ocean_state, ocean_count, regrid_src, regrid_w, dw_kernel,
    atm_gain, atm_up, atm_down, ocean_gain, ocean_up, ocean_down,
):
    tiles = lax.axis_size("tile")

    def move(x, to):
        route = []
        for t in range(tiles):
            for c in range(2):
                u, d = to(t, c)
                if 0 <= u < tiles:
                    route.append((t * 2 + c, u * 2 + d))
        return lax.ppermute(x, AXES, route)

    def partner(x):
        return move(x, lambda t, c: (t, 1 - c))

    half_turn = 8 if tiles >= 16 else 0

    def across(x):
        return move(x, lambda t, c: (t ^ half_turn, 1 - c))

    blocks, blocks_sent = call(
        turn_kernel,
        [sds((1024, 256))] * 2,
        (atm_up, atm_down),
        [ANY] * 2,
        [pltpu.VMEM(v.shape, v.dtype) for v in (atm_up, atm_down)] + [pltpu.SemaphoreType.DMA((2,))],
        name="turn",
    )
    got_blocks = across(blocks_sent)
    ocean_theirs = partner(ocean_state)
    head_sent, own_p, *sends, keep = call(
        open_kernel,
        [sds((HALF + 16, COLS)), sds((16, HALF), F32)]
        + [sds((b - a, HALF, COLS)) for a, b in SENT]
        + [sds((9, HALF, COLS))],
        (atm_state, dw_kernel, atm_gain, ocean_gain),
        [ANY] * 4,
        [pltpu.VMEM(v.shape, v.dtype) for v in (atm_state, dw_kernel, atm_gain, ocean_gain)]
        + [pltpu.SemaphoreType.DMA((5,))],
        name="open",
        flops=4 * 10**9,
    )
    head = partner(head_sent)
    cells = ocean_state.shape[1]
    ocean_kept, ocean_sent, pair, last_sent = call(
        ocean_kernel,
        [sds((HALF, cells), F32), sds((HALF, cells)), sds((2, HALF, COLS)), sds(sends[-1].shape)],
        (ocean_state, ocean_theirs, own_p, head, keep, ocean_up, ocean_down, blocks, sends[-1]),
        [ANY] + [WHOLE] * 4 + [ANY] * 4,
        [pltpu.VMEM((256, cells), BF16)]
        + [pltpu.VMEM(v.shape, v.dtype) for v in (ocean_state, ocean_up, ocean_down)]
        + [pltpu.SemaphoreType.DMA((3,))],
        out_specs=[WHOLE] * 3 + [ANY],
        input_output_aliases={8: 3},
        name="ocean",
        flops=OCEAN_COST,
    )
    ocean_got = partner(ocean_sent)
    edges = move(pair, lambda t, c: (t - 1 + 2 * ((t + c) % 2), c))
    ocean_result, slots = call(
        ocean_result_kernel,
        [sds((HALF, cells)), sds((SLOTS, HALF, CELLS_PER_TILE))],
        (ocean_count, ocean_state, ocean_kept, ocean_got),
        [SMEM, WHOLE, WHOLE, WHOLE],
        name="result",
    )
    got = [partner(s) for s in (*sends[:-1], last_sent)]
    swapped = move(slots, lambda t, c: (t ^ 1, c))
    kept_rows, got_rows = [], []
    for a, b in MIXED:
        ins, own_lines, other_lines = [keep], [], []
        for j in range(a - 1, b + 1):
            if j < 0:
                own_lines.append((len(ins), 0))
                other_lines.append((len(ins), 1))
                ins.append(edges)
                continue
            own_lines.append((0, j))
            if j == 0:
                other_lines.append((len(ins), None))
                ins.append(head)
                continue
            k = [n for n, (p, q) in enumerate(SENT) if p <= j < q][0]
            place = [n for n, x in enumerate(ins) if x is got[k]] or [len(ins)]
            ins += [got[k]] * (place[0] == len(ins))
            other_lines.append((place[0], j - SENT[k][0]))
        rows, leads = b - a, not kept_rows
        order = (edges, got[-1]) if leads else ()
        kept, sent = call(
            functools.partial(mix_kernel, rows, own_lines, other_lines, len(ins), len(order)),
            [sds((rows, HALF, COLS))] * 2,
            (own_p, head, blocks, got_blocks, *ins, *order),
            [WHOLE] * (4 + len(ins)) + [ANY] * len(order),
            [pltpu.VMEM((CHANNELS, rows * COLS), BF16)],
            name="mix",
            flops=MIX_COST if leads else 0,
        )
        kept_rows.append(kept)
        got_rows.append(partner(sent))
    e2 = move(slots, lambda t, c: (t ^ 2, c))
    e1 = move(slots, lambda t, c: (t + 2 if t // 2 % 2 else t - 2, c))
    swap_e1, swap_e2 = [move(e, lambda t, c: (t ^ 1, c)) for e in (e1, e2)]

    steps = 2
    per_step = regrid_src.shape[0] // steps
    table = pl.BlockSpec((SLOTS, HALF, CELLS_PER_TILE), lambda i: (0, 0, 0))
    regrid = call(
        regrid_kernel,
        sds((ROWS, HALF, COLS)),
        (regrid_src.T, slots, swapped, e1, e2, swap_e1, swap_e2, regrid_w, got_rows[0]),
        [SMEM] + [table] * 6 + [pl.BlockSpec((per_step, 2, 128, 128), lambda i: (i, 0, 0, 0)), ANY],
        [pltpu.VMEM((6 * SLOTS, HALF, CELLS_PER_TILE), BF16)],
        grid=(steps,),
        out_specs=pl.BlockSpec((ROWS // steps, HALF, COLS), lambda i: (i, 0, 0)),
        name="regrid",
    )
    depth = HALF // FINAL_STEPS
    rows_spec = [pl.BlockSpec((b - a, depth, COLS), lambda i: (0, i, 0)) for a, b in MIXED]
    state_spec = pl.BlockSpec((depth, ROWS, COLS), lambda i: (i, 0, 0))
    atm_out = call(
        functools.partial(final_kernel, len(MIXED)),
        sds((HALF, ROWS, COLS)),
        (atm_state, regrid, *kept_rows, *got_rows),
        [state_spec, pl.BlockSpec((ROWS, depth, COLS), lambda i: (0, i, 0))] + rows_spec * 2,
        grid=(FINAL_STEPS,),
        out_specs=state_spec,
        name="final",
    )
    return (atm_out, ocean_result)


def solution(mesh):
    return jax.shard_map(
        on_device,
        mesh=mesh,
        in_specs=(
            P("comp", "tile", None),
            P("comp", "tile"),
            P("tile"),
            P("tile", None),
            P("tile", None, None, None),
            P(None, "comp"),
            P("comp"),
            P(None, "comp"),
            P("comp", None),
            P("comp"),
            P(None, "comp"),
            P("comp", None),
        ),
        out_specs=(P("comp", "tile", None), P("comp", "tile")),
        check_vma=False,
    )
```
